32 devices in a mesh: grp: 4 (over y, core), tok: 8 (over z, x).
Axes of the slice: x: 2, y: 2, z: 4, core: 2. Of those that a mesh axis runs over, the one named last changes fastest.
Arguments:
- tokens: bfloat16 [4, 1024, 1280], P('grp', 'tok'), may hold values from -6 to 6
- seg_lengths: int32 [4, 16], P('grp'), may hold values from 1 to 256, 1024 in all within a row
- prefix_keys: bfloat16 [4, 2048, 1280], P('grp', 'tok'), may hold values from -6 to 6
- prefix_values: bfloat16 [4, 2048, 1280], P('grp', 'tok'), may hold values from -0.4375 to 0.4375
- w_qkv: bfloat16 [1280, 3840], replicated, may hold values from -0.15625 to 0.15625
- w_out: bfloat16 [1280, 1280], replicated, may hold values from -0.15625 to 0.15625
- qk_scale: float32 [1280], replicated, may hold values from 0.3 to 10
- attn_rate: float32 [1280], replicated, may hold values from 0.05 to 0.5
- w_up: bfloat16 [1280, 5120], P(None, 'grp'), may hold values from -0.15625 to 0.15625
- w_gate: bfloat16 [1280, 5120], P(None, 'grp'), may hold values from -0.15625 to 0.15625
- w_down: bfloat16 [5120, 1280], P('grp'), may hold values from -0.078125 to 0.078125
- up_scale: float32 [5120], P('grp'), may hold values from 0.5 to 2
- gate_scale: float32 [5120], P('grp'), may hold values from 0.5 to 2
- mlp_rate: float32 [1280], replicated, may hold values from 0.05 to 0.5
Outputs:
- mixed: bfloat16 [4, 1024, 1280], P('grp', 'tok')
The draws below stay inside these ranges and needn't reach their ends.
Inputs may be any that keep to these rules, and one draw needn't show every extreme that they name: `seg_lengths`: row g lists the lengths of group g's 16 requests in order of position; they sum to 1024 and the longest is exactly 256.
All inputs are finite; a program needn't handle non-finite values.
Results may differ from the reference program's by a relative error of at most 0.0085.
The reference program's roundings to bfloat16 on the way count: a program that leaves them out, or rounds other values in their place, can miss the bound.
Values may be sent and summed in bfloat16 or wider, within the bound.
No kernel may reach another device: no remote copies, remote signals or barrier semaphores. Data moves between devices by JAX's collectives and lax.ppermute only.
A program may use at most 128 MiB of HBM per device.

```python
import math
import jax
import jax.numpy as jnp
import numpy as np
from jax import lax

D = 1280
HEADS = 20
HEAD = 64
FF = 5120
TOK_DEV = 128
PREFIX_DEV = 256
SUFFIX = 1024
PREFIX = 2048
REQS = 16
N_GRP = 4
N_TOK = 8


def draw_qk_scale(key, part):
    scales = jnp.exp(jax.random.uniform(jax.random.fold_in(key, 5), (D,), minval=math.log(0.3), maxval=math.log(3.0)))
    scales = jnp.clip(scales, 0.3, 3.0)
    return scales.astype(jnp.float32)


def draw_prefix_keys(key, part):
    result = jnp.clip(jax.random.normal(jax.random.fold_in(key, 8), (N_GRP, PREFIX, D)), -6.0, 6.0)
    return result.astype(jnp.bfloat16)


def block_levels(own_key, extent, cuts, low, high):
    gain = 1.0
    for axis_at, blocks in cuts:
        draws = jax.random.uniform(jax.random.fold_in(jax.random.fold_in(own_key, 6), axis_at), (blocks,), jnp.float32, low / len(cuts), high / len(cuts))
        gain = gain * jnp.repeat(jnp.exp(draws), extent[axis_at] // blocks).reshape((-1,) + (1,) * (len(extent) - 1 - axis_at))
    return gain


def split_up(amount, total, bound, skew):
    portions = [(1 << 20) // math.isqrt(rank ** skew) + 1 for rank in range(2, amount + 1)]
    spare, counts = total - bound - (amount - 1), [1] * (amount - 1)
    while spare > 0:
        free = [i for i in range(amount - 1) if counts[i] < bound]
        whole, budget = sum([portions[i] for i in free]), spare
        for i in free:
            more = min(bound - counts[i], max(1, budget * portions[i] // whole), spare)
            counts[i] = counts[i] + more
            spare = spare - more
    return np.array([bound] + counts)


def uneven(rng, number_of, total, bound, slope):
    if number_of == 2:
        one = jax.random.randint(rng, (), max(1, total - bound), min(bound, total - 1) + 1)
        return jnp.stack([one, total - one])
    sizes = jnp.asarray(split_up(number_of, total, bound, slope), jnp.int32)
    couples = (number_of - 1) // 2
    source_of, sink = sizes[1:1 + 2 * couples:2], sizes[2:2 + 2 * couples:2]
    slack = jnp.minimum(source_of - 1, bound - sink)
    passed = jax.random.randint(jax.random.fold_in(rng, 1), (couples,), 0, 1 << 20) % (slack + 1)
    sizes = sizes.at[1:1 + 2 * couples:2].set(source_of - passed).at[2:2 + 2 * couples:2].set(sink + passed)
    return sizes[jax.random.permutation(jax.random.fold_in(rng, 2), number_of)]


def noise(key, extent, width, bound, shards=(), kind=jnp.bfloat16):
    array = jax.random.normal(key, extent, jnp.float32) * width
    if len(shards) > 0:
        array = block_levels(key, extent, shards, -0.22, 0.18) * array
    return jnp.clip(array, min=-bound, max=bound).astype(kind)


def setup_inputs(seed: int = 0) -> dict:
    key_of = jax.random.split(jax.random.key(seed), 15)
    return {
        "tokens": noise(key_of[0], (N_GRP, SUFFIX, D), 1.0, 6.0, ((0, 4), (1, 8))),
        "seg_lengths": jax.vmap(lambda own: uneven(own, REQS, SUFFIX, 2 * TOK_DEV, 2))(jax.random.split(key_of[1], N_GRP)).reshape((N_GRP, REQS)).astype(jnp.int32),
        "prefix_keys": draw_prefix_keys(jax.random.fold_in(key_of[14], 71), 0),
        "prefix_values": noise(key_of[3], (N_GRP, PREFIX, D), (D ** -0.5), 0.4375, ((0, 4), (1, 8))),
        "w_qkv": noise(key_of[4], (D, 3 * D), D ** -0.5, 0.15625),
        "w_out": noise(key_of[5], (D, D), D ** -0.5, 0.15625),
        "qk_scale": draw_qk_scale(jax.random.fold_in(key_of[14], 71), 0),
        "attn_rate": jnp.clip(jnp.exp(jax.random.uniform(key_of[7], (D,), jnp.float32, math.log(0.05), math.log(0.5))), 0.05, 0.5),
        "w_up": noise(key_of[8], (D, FF), D ** -0.5, 0.15625, ((1, 4),)),
        "w_gate": noise(key_of[9], (D, FF), D ** -0.5, 0.15625, ((1, 4),)),
        "w_down": noise(key_of[10], (FF, D), FF ** -0.5, 0.078125, ((0, 4),)),
        "up_scale": jnp.clip(jnp.exp(math.log(2.0) - 1.3862944 * jax.random.uniform(key_of[11], (FF,), jnp.float32) ** block_levels(key_of[11], (FF,), ((0, 4),), -0.2, 0.2)), 0.5, 2.0),
        "gate_scale": jnp.clip(jnp.exp(math.log(2.0) - 1.3862944 * jax.random.uniform(key_of[12], (FF,), jnp.float32) ** block_levels(key_of[12], (FF,), ((0, 4),), -0.2, 0.2)), 0.5, 2.0),
        "mlp_rate": jnp.clip(jnp.exp(jax.random.uniform(key_of[13], (D,), jnp.float32, math.log(0.05), math.log(0.5))), 0.05, 0.5),
    }


EPS = 1e-06

def unit(vector):
    return vector * lax.rsqrt(lax.optimization_barrier(jnp.sum(vector * vector, axis=-1, keepdims=True)) + EPS)

def head_unit(vector, scaling):
    per_head = vector.reshape(vector.shape[0], HEADS, HEAD)
    return unit(per_head) * scaling.reshape(HEADS, HEAD)

def segment_of(position, lengths):
    bounds = jnp.cumsum(lengths, dtype=jnp.int32)
    return lax.optimization_barrier(jnp.sum((position[:, None] >= bounds[None, :]).astype(jnp.int32), axis=1)).astype(jnp.int32)

def block_state(query, keys, values, allowed):
    scores = math.sqrt(HEAD) * jnp.einsum('rhd,khd->rhk', query.astype(jnp.float32), keys.astype(jnp.float32))
    if allowed is not None:
        scores = jnp.where(allowed[:, None, :], scores, -jnp.inf)
    maximum = lax.optimization_barrier(jnp.max(scores, axis=-1))
    weights = jnp.exp(scores - maximum[..., None])
    totals = lax.optimization_barrier(jnp.sum(weights, axis=-1))
    rounded = lax.optimization_barrier(weights.astype(jnp.bfloat16))
    blended = jnp.einsum('rhk,khd->rhd', rounded.astype(jnp.float32), values.astype(jnp.float32))
    return ((blended / totals[..., None]).astype(jnp.bfloat16), maximum, totals)

def start_state(block):
    blended, maximum, totals = block
    return (maximum, totals, totals[..., None] * blended.astype(jnp.float32))

def merge_block(running, block):
    maximum, totals, accum = running
    blended, block_max, block_sum = block
    new_max = jnp.maximum(maximum, block_max)
    shrink_old = jnp.exp(maximum - new_max)
    weight_new = jnp.exp(block_max - new_max) * block_sum
    return (new_max, totals * shrink_old + weight_new, accum * shrink_old[..., None] + weight_new[..., None] * blended.astype(jnp.float32))

def one_group(tokens, lengths, prefix_keys, prefix_values, w_qkv, w_out, qk_scale, attn_rate, w_up, w_gate, w_down, up_scale, gate_scale, mlp_rate):
    hidden_state = unit(tokens.astype(jnp.float32))
    projected = jnp.dot(hidden_state.astype(jnp.bfloat16), w_qkv, preferred_element_type=jnp.float32)
    query = head_unit(projected[:, :D], qk_scale).astype(jnp.bfloat16)
    suffix_keys = head_unit(projected[:, D:2 * D], qk_scale).astype(jnp.bfloat16)
    suffix_values = projected[:, 2 * D:].astype(jnp.bfloat16).reshape(SUFFIX, HEADS, HEAD)
    cached_keys = head_unit(prefix_keys.astype(jnp.float32), qk_scale).astype(jnp.bfloat16)
    cached_values = prefix_values.reshape(PREFIX, HEADS, HEAD)
    position = jnp.arange(SUFFIX, dtype=jnp.int32)
    segment = segment_of(position, lengths)
    margin = 2 * TOK_DEV
    keys_pad = jnp.concatenate([jnp.zeros((margin, HEADS, HEAD), jnp.bfloat16), suffix_keys], axis=0)
    values_pad = jnp.concatenate([jnp.zeros((margin, HEADS, HEAD), jnp.bfloat16), suffix_values], axis=0)
    pos_pad = jnp.concatenate([jnp.arange(-margin, 0, dtype=jnp.int32), position])
    seg_pad = jnp.concatenate([jnp.full((margin,), -1, jnp.int32), segment])

    def local_block(block_index):
        begin = (block_index * TOK_DEV).astype(jnp.int32)
        query_rows = lax.dynamic_slice_in_dim(query, begin, TOK_DEV, 0)
        key_rows = lax.dynamic_slice_in_dim(keys_pad, begin, 3 * TOK_DEV, 0)
        value_rows = lax.dynamic_slice_in_dim(values_pad, begin, 3 * TOK_DEV, 0)
        key_pos = lax.dynamic_slice_in_dim(pos_pad, begin, 3 * TOK_DEV, 0)
        key_seg = lax.dynamic_slice_in_dim(seg_pad, begin, 3 * TOK_DEV, 0)
        query_pos = lax.dynamic_slice_in_dim(position, begin, TOK_DEV, 0)
        query_seg = lax.dynamic_slice_in_dim(segment, begin, TOK_DEV, 0)
        allowed = (key_seg[None, :] == query_seg[:, None]) & (key_pos[None, :] <= query_pos[:, None]) & (key_pos[None, :] >= 0)
        return block_state(query_rows, key_rows, value_rows, allowed)
    local = lax.map(local_block, jnp.arange(N_TOK, dtype=jnp.int32))
    local = (local[0].reshape(SUFFIX, HEADS, HEAD), local[1].reshape(SUFFIX, HEADS), local[2].reshape(SUFFIX, HEADS))
    shard_keys = cached_keys.reshape(N_TOK, PREFIX_DEV, HEADS, HEAD)
    shard_values = cached_values.reshape(N_TOK, PREFIX_DEV, HEADS, HEAD)

    def add_shard(running, matched):
        return (merge_block(running, block_state(query, matched[0], matched[1], None)), None)
    final, ignored = lax.scan(add_shard, start_state(local), (shard_keys, shard_values))
    maximum, totals, accum = final
    attn_mix = (accum / totals[..., None]).astype(jnp.bfloat16).reshape(SUFFIX, D)
    attended = unit(jnp.dot(attn_mix, w_out, preferred_element_type=jnp.float32))
    hidden_state = unit(hidden_state + attn_rate * (attended - hidden_state))
    flattened = hidden_state.astype(jnp.bfloat16)
    up_part = jnp.dot(flattened, w_up, preferred_element_type=jnp.float32) * up_scale
    gate_part = jnp.dot(flattened, w_gate, preferred_element_type=jnp.float32) * (gate_scale * math.sqrt(D))
    act = (up_part * jax.nn.silu(gate_part)).astype(jnp.bfloat16)
    mlp_dir = unit(jnp.dot(act, w_down, preferred_element_type=jnp.float32))
    hidden_state = unit(hidden_state + mlp_rate * (mlp_dir - hidden_state))
    return (math.sqrt(D) * hidden_state).astype(jnp.bfloat16)

def reference(tokens, seg_lengths, prefix_keys, prefix_values, w_qkv, w_out, qk_scale, attn_rate, w_up, w_gate, w_down, up_scale, gate_scale, mlp_rate):

    def one_pass(group_items):
        return one_group(group_items[0], group_items[1], group_items[2], group_items[3], w_qkv, w_out, qk_scale, attn_rate, w_up, w_gate, w_down, up_scale, gate_scale, mlp_rate)
    return lax.map(one_pass, (tokens, seg_lengths, prefix_keys, prefix_values))
```

```python
import functools
import math

import jax
import jax.numpy as jnp
from jax import lax
from jax.experimental import pallas as pl
from jax.experimental.pallas import tpu as pltpu
from jax.sharding import PartitionSpec as P

D = 1280
HEADS = 20
HEAD = 64
EPS = 1e-06
SQ = 4
HQ = HEADS // SQ
QD = HQ * HEAD
LSE = 32
NEG = -1e30
MIB = 1 << 20

f32 = jnp.float32
bf16 = jnp.bfloat16


def unit(vector):
    return vector * lax.rsqrt(jnp.sum(vector * vector, axis=-1, keepdims=True) + EPS)


def head_unit_t(block, scale):
    dims, rows = block.shape
    per_head = block.reshape(dims // HEAD, HEAD, rows)
    total = jnp.sum(per_head * per_head, axis=1, keepdims=True)
    return (per_head * lax.rsqrt(total + EPS)).reshape(dims, rows) * scale


def params(limit=48):
    return pltpu.CompilerParams(vmem_limit_bytes=limit * MIB)


def vmem():
    return pl.BlockSpec(memory_space=pltpu.VMEM)


def smem():
    return pl.BlockSpec(memory_space=pltpu.SMEM)


def cost(flops, nbytes, trans=0):
    return pl.CostEstimate(flops=int(flops), bytes_accessed=int(nbytes), transcendentals=int(trans))


def quarter(i, m):
    return pl.multiple_of(jnp.bitwise_xor(i, m) * QD, QD)


def prefix_kernel(place, keys, values, scale, *rest):
    outs, scratch = rest[:SQ], rest[SQ]
    rows = keys.shape[0]
    i = lax.rem(place[0], SQ)
    for c in range(D // 128):
        cols = slice(c * 128, (c + 1) * 128)
        scale_t = jnp.broadcast_to(scale[:, cols], (128, 128)).T
        scale_t = jnp.concatenate([scale_t] * (rows // 128), axis=1)
        key_t = keys[:, cols].astype(f32).T
        scratch[cols, :] = head_unit_t(key_t, scale_t).astype(bf16)
        scratch[D + c * 128 : D + (c + 1) * 128, :] = values[:, cols].astype(f32).T.astype(bf16)
    for m in range(SQ):
        at = quarter(i, m)
        outs[m][:QD, :] = scratch[pl.ds(at, QD), :]
        outs[m][QD:, :] = scratch[pl.ds(D + at, QD), :]


def prefix_call(place, keys, values, scale):
    rows = keys.shape[0]
    return pl.pallas_call(
        prefix_kernel,
        out_shape=[jax.ShapeDtypeStruct((2 * QD, rows), bf16)] * SQ,
        in_specs=[smem(), vmem(), vmem(), vmem()],
        out_specs=[vmem()] * SQ,
        scratch_shapes=[pltpu.VMEM((2 * D, rows), bf16)],
        compiler_params=params(),
        cost_estimate=cost(0, 4 * rows * D * 2),
        name="prefix_prep",
    )(place, keys, values, scale)


QKV_BLOCK = 640


def qkv_kernel(place, tokens, weights, scale, *rest):
    full, query_outs, (hidden, scratch) = rest[:SQ], rest[SQ : 2 * SQ], rest[2 * SQ :]
    step = pl.program_id(0)
    per_part = D // QKV_BLOCK

    @pl.when(step == 0)
    def _():
        hidden[...] = unit(tokens[...].astype(f32)).astype(bf16)

    out = jnp.dot(hidden[...], weights[...], preferred_element_type=f32)
    at = pl.multiple_of(step * QKV_BLOCK, QKV_BLOCK)

    @pl.when(step < 2 * per_part)
    def _():
        times = jnp.where(step < per_part, math.sqrt(HEAD), 1.0)
        for c in range(QKV_BLOCK // 128):
            cols = slice(c * 128, (c + 1) * 128)
            scale_t = jnp.broadcast_to(scale[:, cols], (128, 128)).T
            block = head_unit_t(out[:, cols].T, scale_t[:, : out.shape[0]])
            scratch[pl.ds(at + c * 128, 128), :] = (block * times).astype(bf16)

    @pl.when(step >= 2 * per_part)
    def _():
        for c in range(QKV_BLOCK // 128):
            scratch[pl.ds(at + c * 128, 128), :] = out[:, c * 128 : (c + 1) * 128].T.astype(bf16)

    @pl.when(step == 3 * per_part - 1)
    def _():
        i = lax.rem(place[0], SQ)
        for m in range(SQ):
            start = quarter(i, m)
            query_outs[m][...] = scratch[pl.ds(start, QD), :]
            for part in range(3):
                full[m][part * QD : (part + 1) * QD, :] = scratch[pl.ds(part * D + start, QD), :]


def qkv_call(place, tokens, weights, scale):
    rows = tokens.shape[0]
    per_part = D // QKV_BLOCK
    whole = lambda j, place: (0, 0)
    return pl.pallas_call(
        qkv_kernel,
        out_shape=[jax.ShapeDtypeStruct((3 * QD, rows), bf16)] * SQ
        + [jax.ShapeDtypeStruct((QD, rows), bf16)] * SQ,
        grid_spec=pltpu.PrefetchScalarGridSpec(
            num_scalar_prefetch=1,
            grid=(3 * per_part,),
            in_specs=[
                pl.BlockSpec((rows, D), whole),
                pl.BlockSpec((D, QKV_BLOCK), lambda j, place: (0, j)),
                pl.BlockSpec((1, QKV_BLOCK), lambda j, place: (0, lax.rem(j, per_part))),
            ],
            out_specs=[pl.BlockSpec((3 * QD, rows), whole)] * SQ
            + [pl.BlockSpec((QD, rows), whole)] * SQ,
            scratch_shapes=[pltpu.VMEM((rows, D), bf16), pltpu.VMEM((3 * D, rows), bf16)],
        ),
        compiler_params=params(),
        cost_estimate=cost(2 * rows * D * 3 * D, 3 * D * D * 2),
        name="qkv",
    )(place, tokens, weights, scale)


def block_state(score, values_t):
    top = jnp.max(score, axis=0, keepdims=True)
    weights = jnp.exp(score - top)
    total = jnp.sum(weights, axis=0, keepdims=True)
    blended = jnp.dot(values_t, weights.astype(bf16), preferred_element_type=f32)
    return (blended * (1.0 / total)).astype(bf16).astype(f32), top, total


def merge(states):
    top = functools.reduce(jnp.maximum, [s[1] for s in states])
    weights = [jnp.exp(s[1] - top) * s[2] for s in states]
    total = functools.reduce(jnp.add, weights)
    accum = functools.reduce(jnp.add, [w * s[0] for w, s in zip(weights, states)])
    return accum * (1.0 / total), top + jnp.log(total)


def attend_kernel(shift, place, lengths, *rest):
    suffix = rest[:SQ]
    prefix = rest[SQ : 2 * SQ]
    rest = rest[2 * SQ :]
    if shift:
        queries, rest = rest[:SQ], rest[SQ:]
    else:
        queries = suffix
    outs, (query, keys, values, out, lse) = rest[:SQ], rest[SQ:]
    rows = suffix[0].shape[1]
    i = lax.rem(place[0], SQ)
    square = lax.div(place[0], SQ)
    query_square = jnp.bitwise_xor(square, shift)
    for m in range(SQ):
        lanes = pl.ds(pl.multiple_of(jnp.bitwise_xor(i, m) * rows, rows), rows)
        query[:, lanes] = queries[m][:QD, :]
        keys[:, lanes] = suffix[m][QD : 2 * QD, :]
        values[:, lanes] = suffix[m][2 * QD :, :]
    lse[...] = jnp.zeros_like(lse)

    position = query_square * (SQ * rows) + lax.broadcasted_iota(jnp.int32, (1, SQ * rows), 1)
    first = jnp.zeros((1, SQ * rows), jnp.int32)
    bound = jnp.int32(0)
    for r in range(lengths.shape[1]):
        bound = bound + lengths[0, r]
        first = jnp.where(position >= bound, bound, first)

    def own(h, j, key_from, key_to):
        head = slice(h * HEAD, (h + 1) * HEAD)
        lanes = slice(j * rows, (j + 1) * rows)
        span = slice(key_from * rows, key_to * rows)
        score = jnp.dot(
            keys[head, span].astype(f32).T.astype(bf16), query[head, lanes], preferred_element_type=f32
        )
        key_at = (square * SQ + key_from) * rows + lax.broadcasted_iota(jnp.int32, score.shape, 0)
        allowed = (key_at >= first[:, lanes]) & (key_at <= position[:, lanes])
        return block_state(jnp.where(allowed, score, NEG), values[head, span])

    def run(with_suffix):
        for h in range(HQ):
            head = slice(h * HEAD, (h + 1) * HEAD)
            head_v = slice(QD + h * HEAD, QD + (h + 1) * HEAD)
            keys_n = [prefix[m][head, :].astype(f32).T.astype(bf16) for m in range(SQ)]
            for c in range(0, SQ, 2):
                lanes = slice(c * rows, (c + 2) * rows)
                states = [
                    block_state(
                        jnp.dot(keys_n[m], query[head, lanes], preferred_element_type=f32),
                        prefix[m][head_v, :],
                    )
                    for m in range(SQ)
                ]
                extra = None
                if with_suffix and not shift:
                    extra = [own(h, j, max(0, j - 2), j + 1) for j in (c, c + 1)]
                elif with_suffix and c == 0:
                    extra = [own(h, j, SQ - 2 + j, SQ) for j in (0, 1)]
                if extra:
                    states.append(tuple(jnp.concatenate(p, axis=1) for p in zip(*extra)))
                mixed, level = merge(states)
                out[head, lanes] = mixed.astype(bf16)
                lse[h : h + 1, lanes] = level

    if shift:
        follows = query_square == square + 1
        pl.when(follows)(lambda: run(True))
        pl.when(jnp.logical_not(follows))(lambda: run(False))
    else:
        run(True)

    level = lse[...]
    high = level.astype(bf16).astype(f32)
    middle = (level - high).astype(bf16).astype(f32)
    low = level - high - middle
    pieces = jnp.concatenate([high, middle, low, jnp.zeros_like(low)], axis=0).astype(bf16)
    out[QD:, :] = pieces
    for m in range(SQ):
        lanes = pl.ds(pl.multiple_of(jnp.bitwise_xor(i, m) * rows, rows), rows)
        outs[m][...] = out[:, lanes]


def attend_call(shift, place, lengths, suffix, prefix, queries):
    rows = suffix[0].shape[1]
    span = prefix[0].shape[1]
    ins = [*suffix, *prefix, *queries]
    pairs = SQ * rows * SQ * span * HQ
    return pl.pallas_call(
        functools.partial(attend_kernel, shift),
        out_shape=[jax.ShapeDtypeStruct((QD + LSE, rows), bf16)] * SQ,
        in_specs=[smem(), smem()] + [vmem()] * len(ins),
        out_specs=[vmem()] * SQ,
        scratch_shapes=[
            pltpu.VMEM((QD, SQ * rows), bf16),
            pltpu.VMEM((QD, SQ * rows), bf16),
            pltpu.VMEM((QD, SQ * rows), bf16),
            pltpu.VMEM((QD + LSE, SQ * rows), bf16),
            pltpu.VMEM((8, SQ * rows), f32),
        ],
        compiler_params=params(),
        cost_estimate=cost(4 * 4 * HEAD * pairs, 4 * MIB, pairs),
        name="attend_cross" if shift else "attend_own",
    )(place, lengths, *ins)


def project_kernel(count, place, tokens, rate, w_hbm, *rest):
    parts = rest[: SQ * count]
    hidden_out, flat_out, mix, w_out, sem = rest[SQ * count :]
    copy = pltpu.make_async_copy(w_hbm, w_out, sem)
    copy.start()
    i = lax.rem(place[0], SQ)
    for m in range(SQ):
        group = [parts[s * SQ + m] for s in range(count)]
        levels = []
        for part in group:
            pieces = part[QD:, :].astype(f32)
            levels.append(pieces[0:8, :] + pieces[8:16, :] + pieces[16:24, :])
        top = functools.reduce(jnp.maximum, levels)
        weights = [jnp.exp(v - top) for v in levels]
        inverse = 1.0 / functools.reduce(jnp.add, weights)
        weights = [w * inverse for w in weights]
        start = quarter(i, m)
        for h in range(HQ):
            head = slice(h * HEAD, (h + 1) * HEAD)
            mixed = functools.reduce(
                jnp.add, [w[h : h + 1, :] * p[head, :].astype(f32) for w, p in zip(weights, group)]
            )
            mix[pl.ds(start + h * HEAD, HEAD), :] = mixed.astype(bf16)
    hidden = unit(tokens[...].astype(f32))
    attn = jnp.concatenate(
        [mix[c * 128 : (c + 1) * 128, :].astype(f32).T.astype(bf16) for c in range(D // 128)], axis=1
    )
    copy.wait()
    attended = unit(jnp.dot(attn, w_out[...], preferred_element_type=f32))
    hidden = unit(hidden + rate[...] * (attended - hidden))
    hidden_out[...] = hidden
    flat_out[...] = hidden.astype(bf16)


def project_call(place, tokens, rate, w_out, parts):
    rows = tokens.shape[0]
    return pl.pallas_call(
        functools.partial(project_kernel, len(parts) // SQ),
        out_shape=[jax.ShapeDtypeStruct((rows, D), f32), jax.ShapeDtypeStruct((rows, D), bf16)],
        in_specs=[smem(), vmem(), vmem(), pl.BlockSpec(memory_space=pl.ANY)] + [vmem()] * len(parts),
        out_specs=[vmem()] * 2,
        scratch_shapes=[
            pltpu.VMEM((D, rows), bf16),
            pltpu.VMEM((D, D), bf16),
            pltpu.SemaphoreType.DMA,
        ],
        compiler_params=params(),
        cost_estimate=cost(2 * rows * D * D, D * D * 2),
        name="project",
    )(place, tokens, rate, w_out, *parts)


FF_BLOCK = 256


def mlp_kernel(first, second, w_up, w_gate, w_down, up_scale, gate_scale, keep, send, rows_in, total):
    step = pl.program_id(0)
    rows = first.shape[0]

    @pl.when(step == 0)
    def _():
        rows_in[:rows, :] = first[...]
        rows_in[rows:, :] = second[...]

    data = rows_in[...]
    up = jnp.dot(data, w_up[...], preferred_element_type=f32) * up_scale[...]
    gate = jnp.dot(data, w_gate[...], preferred_element_type=f32) * (gate_scale[...] * math.sqrt(D))
    act = (up * (gate / (1.0 + jnp.exp(-gate)))).astype(bf16)
    part = jnp.dot(act, w_down[...], preferred_element_type=f32)

    @pl.when(step == 0)
    def _():
        total[...] = part

    @pl.when(step > 0)
    def _():
        total[...] += part

    @pl.when(step == pl.num_programs(0) - 1)
    def _():
        keep[...] = total[:rows, :]
        send[...] = total[rows:, :].astype(bf16)


def mlp_call(first, second, w_up, w_gate, w_down, up_scale, gate_scale):
    rows = first.shape[0]
    units = w_up.shape[1]
    whole = lambda j: (0, 0)
    across = lambda j: (0, j)
    return pl.pallas_call(
        mlp_kernel,
        grid=(units // FF_BLOCK,),
        out_shape=[jax.ShapeDtypeStruct((rows, D), f32), jax.ShapeDtypeStruct((rows, D), bf16)],
        in_specs=[
            pl.BlockSpec((rows, D), whole),
            pl.BlockSpec((rows, D), whole),
            pl.BlockSpec((D, FF_BLOCK), across),
            pl.BlockSpec((D, FF_BLOCK), across),
            pl.BlockSpec((FF_BLOCK, D), lambda j: (j, 0)),
            pl.BlockSpec((1, FF_BLOCK), across),
            pl.BlockSpec((1, FF_BLOCK), across),
        ],
        out_specs=[pl.BlockSpec((rows, D), whole)] * 2,
        scratch_shapes=[pltpu.VMEM((2 * rows, D), bf16), pltpu.VMEM((2 * rows, D), f32)],
        compiler_params=params(),
        cost_estimate=cost(2 * 2 * rows * D * units * 3, 3 * D * units * 2, 2 * rows * units),
        name="mlp",
    )(first, second, w_up, w_gate, w_down, up_scale, gate_scale)


def add_kernel(kept, arrived, out):
    out[...] = (kept[...] + arrived[...].astype(f32)).astype(bf16)


def add_call(kept, arrived):
    return pl.pallas_call(
        add_kernel,
        out_shape=jax.ShapeDtypeStruct(kept.shape, bf16),
        in_specs=[vmem()] * 2,
        out_specs=vmem(),
        cost_estimate=cost(kept.size, kept.size * 8),
        name="add_partials",
    )(kept, arrived)


def final_kernel(hidden, rate, kept, *rest):
    arrived, out = rest[:-1], rest[-1]
    total = kept[...]
    for part in arrived:
        total = total + part[...].astype(f32)
    state = hidden[...]
    state = unit(state + rate[...] * (unit(total) - state))
    out[...] = (math.sqrt(D) * state).astype(bf16)


def final_call(hidden, rate, kept, arrived):
    return pl.pallas_call(
        final_kernel,
        out_shape=jax.ShapeDtypeStruct(hidden.shape, bf16),
        in_specs=[vmem()] * (3 + len(arrived)),
        out_specs=vmem(),
        cost_estimate=cost(hidden.size * 10, hidden.size * 12),
        name="finish",
    )(hidden, rate, kept, *arrived)


def swap(shard, axis, mask):
    length = lax.axis_size(axis)
    return lax.ppermute(shard, axis, [(j, j ^ mask) for j in range(length)])


def body(
    tokens,
    seg_lengths,
    prefix_keys,
    prefix_values,
    w_qkv,
    w_out,
    qk_scale,
    attn_rate,
    w_up,
    w_gate,
    w_down,
    up_scale,
    gate_scale,
    mlp_rate,
):
    squares = lax.axis_size("tok") // SQ
    place = lax.axis_index("tok").astype(jnp.int32).reshape(1)
    own = tokens[0]
    scale = qk_scale.reshape(1, D)

    prefix = prefix_call(place, prefix_keys[0], prefix_values[0], scale)
    prefix = [prefix[0]] + [swap(prefix[m], "tok", m) for m in range(1, SQ)]
    sent = qkv_call(place, own, w_qkv, scale)
    suffix = [sent[0]] + [swap(sent[m], "tok", m) for m in range(1, SQ)]
    crossed = [[swap(sent[SQ + m], "tok", SQ * s + m) for m in range(SQ)] for s in range(1, squares)]

    parts = attend_call(0, place, seg_lengths, suffix, prefix, [])
    gathered = [parts[0]] + [swap(parts[m], "tok", m) for m in range(1, SQ)]
    for s in range(1, squares):
        parts = attend_call(s, place, seg_lengths, suffix, prefix, crossed[s - 1])
        gathered += [swap(parts[m], "tok", SQ * s + m) for m in range(SQ)]
    hidden, flat = project_call(place, own, attn_rate.reshape(1, D), w_out, gathered)

    weights = (w_up, w_gate, w_down, up_scale.reshape(1, -1), gate_scale.reshape(1, -1))
    chips = lax.axis_size("grp") // 2
    remote = [swap(flat, "grp", 2 * c) for c in range(1, chips)]
    keep, send = mlp_call(flat, swap(flat, "grp", 1), *weights)
    arrived = [swap(send, "grp", 1)]
    for c in range(1, chips):
        rows = remote[c - 1]
        kept, send = mlp_call(rows, swap(rows, "grp", 1), *weights)
        arrived.append(swap(add_call(kept, swap(send, "grp", 1)), "grp", 2 * c))
    return final_call(hidden, mlp_rate.reshape(1, D), keep, arrived)[None]


def solution(mesh):
    in_specs = (
        P("grp", "tok", None),
        P("grp", None),
        P("grp", "tok", None),
        P("grp", "tok", None),
        P(),
        P(),
        P(),
        P(),
        P(None, "grp"),
        P(None, "grp"),
        P("grp", None),
        P("grp"),
        P("grp"),
        P(),
    )
    out_specs = P("grp", "tok", None)
    return jax.shard_map(body, mesh=mesh, in_specs=in_specs, out_specs=out_specs, check_vma=False)
```

```python
import functools
import math

import jax
import jax.numpy as jnp
from jax import lax
from jax.experimental import pallas as pl
from jax.experimental.pallas import tpu as pltpu
from jax.sharding import PartitionSpec as P

D = 1280
HEADS = 20
HEAD = 64
EPS = 1e-06
SQ = 4
HQ = HEADS // SQ
QD = HQ * HEAD
LSE = 16
NEG = -1e30
MIB = 1 << 20

f32 = jnp.float32
bf16 = jnp.bfloat16


def unit(vector):
    return vector * lax.rsqrt(jnp.sum(vector * vector, axis=-1, keepdims=True) + EPS)


def head_unit_t(block, scale):
    dims, rows = block.shape
    per_head = block.reshape(dims // HEAD, HEAD, rows)
    total = jnp.sum(per_head * per_head, axis=1, keepdims=True)
    return (per_head * lax.rsqrt(total + EPS)).reshape(dims, rows) * scale


def params(limit):
    return pltpu.CompilerParams(vmem_limit_bytes=limit * MIB)


def vmem():
    return pl.BlockSpec(memory_space=pltpu.VMEM)


def hbm():
    return pl.BlockSpec(memory_space=pltpu.HBM)


def fetch(sources, targets, sems):
    copies = [
        pltpu.make_async_copy(a, b, sems.at[n]) for n, (a, b) in enumerate(zip(sources, targets))
    ]
    for copy in copies:
        copy.start()
    return copies


def wait(copies):
    for copy in copies:
        copy.wait()


def fetched(*arrays):
    return [pltpu.VMEM(a.shape, a.dtype) for a in arrays] + [
        pltpu.SemaphoreType.DMA((len(arrays),))
    ]


def over_rows(vector, rows):
    tiles = [
        jnp.broadcast_to(vector[c * 128 : (c + 1) * 128], (rows, 128))
        for c in range(vector.shape[0] // 128)
    ]
    return jnp.concatenate(tiles, axis=1)


def smem():
    return pl.BlockSpec(memory_space=pltpu.SMEM)


def cost(flops, nbytes, trans=0):
    return pl.CostEstimate(flops=int(flops), bytes_accessed=int(nbytes), transcendentals=int(trans))


def prefix_kernel(place, *rest):
    outs, rest, sources = rest[4 : 4 + SQ], rest[4 + SQ :], rest[:4]
    hidden, columns, parts, scale, keys, values, tokens, sems = rest
    copies = fetch(sources, (scale, keys, values, tokens), sems)
    rows = keys.shape[0]
    wait(copies[:2])
    for c in range(D // 128):
        cols = slice(c * 128, (c + 1) * 128)
        columns[c] = jnp.broadcast_to(scale[cols], (128, 128)).T
        scale_t = jnp.concatenate([columns[c]] * (rows // 128), axis=1)
        split(parts, 0, c, head_unit_t(keys[:, cols].T.astype(f32), scale_t).astype(bf16))
    wait(copies[2:])
    for c in range(D // 128):
        split(parts, QD, c, values[:, c * 128 : (c + 1) * 128].T)
    i = lax.rem(place[0], SQ)
    for m in range(SQ):
        outs[m][...] = parts[jnp.bitwise_xor(i, m)]
    hidden[...] = unit(tokens[...].astype(f32)).astype(bf16)


def split(out, base, c, block):
    for part in range(0, 128, HEAD):
        row = c * 128 + part
        at = base + row % QD
        out[row // QD, at : at + HEAD, :] = block[part : part + HEAD, :]


def prefix_call(place, scale, keys, values, tokens):
    rows = keys.shape[0]
    return pl.pallas_call(
        prefix_kernel,
        out_shape=[jax.ShapeDtypeStruct((2 * QD, rows), bf16)] * SQ
        + [
            jax.ShapeDtypeStruct(tokens.shape, bf16),
            jax.ShapeDtypeStruct((D // 128, 128, 128), f32),
        ],
        in_specs=[smem()] + [hbm()] * 4,
        out_specs=[vmem()] * (SQ + 2),
        scratch_shapes=[pltpu.VMEM((SQ, 2 * QD, rows), bf16)]
        + fetched(scale, keys, values, tokens),
        compiler_params=params(6),
        cost_estimate=cost(5e10, 4 * rows * D * 2),
        name="prefix_prep",
    )(place, scale, keys, values, tokens)


def qkv_kernel(squares, place, hidden, columns, w_hbm, queries, *rest):
    outs, (parts, weights, w_sems) = rest[:SQ], rest[SQ:]
    spans = [pl.ds(p * D, D) for p in range(3)]
    copies = fetch([w_hbm.at[:, p] for p in spans], [weights.at[:, p] for p in spans], w_sems)
    rows = hidden.shape[0]
    for part in range(3):
        copies[part].wait()
        out = jnp.dot(hidden[...], weights[:, part * D : (part + 1) * D], preferred_element_type=f32)
        for c in range(D // 128):
            block = out[:, c * 128 : (c + 1) * 128].T
            if part < 2:
                block = head_unit_t(block, columns[c, :, :rows])
            if part == 0:
                block = (block * math.sqrt(HEAD)).astype(bf16)
                for s in range(squares):
                    queries[s * D + c * 128 : s * D + (c + 1) * 128, :] = block
            else:
                split(parts, (part - 1) * QD, c, block.astype(bf16))
    i = lax.rem(place[0], SQ)
    for m in range(SQ):
        outs[m][...] = parts[jnp.bitwise_xor(i, m)]


def qkv_call(squares, place, hidden, columns, weights):
    rows = hidden.shape[0]
    pair = jax.ShapeDtypeStruct((2 * QD, rows), bf16)
    return pl.pallas_call(
        functools.partial(qkv_kernel, squares),
        out_shape=[jax.ShapeDtypeStruct((squares * D, rows), bf16)] + [pair] * SQ,
        in_specs=[smem(), vmem(), vmem(), hbm()],
        out_specs=[vmem()] * (1 + SQ),
        scratch_shapes=[
            pltpu.VMEM((SQ, 2 * QD, rows), bf16),
            pltpu.VMEM((D, 3 * D), bf16),
            pltpu.SemaphoreType.DMA((3,)),
        ],
        compiler_params=params(14),
        cost_estimate=cost(5e10, 3 * D * D * 2),
        name="qkv",
    )(place, hidden, columns, weights)


def pack_kernel(*refs):
    parts, (keys, values) = refs[:SQ], refs[SQ:]
    span = parts[0].shape[1]
    for n, part in enumerate(parts):
        at = slice(n * span, (n + 1) * span)
        for h in range(HQ):
            keys[h, at, :] = part[h * HEAD : (h + 1) * HEAD, :].T
        values[:, at] = part[QD:, :]


PACK_COST = 20e9


def pack_call(parts):
    span = parts[0].shape[1]
    return pl.pallas_call(
        pack_kernel,
        out_shape=[
            jax.ShapeDtypeStruct((HQ, SQ * span, HEAD), bf16),
            jax.ShapeDtypeStruct((QD, SQ * span), bf16),
        ],
        in_specs=[vmem()] * SQ,
        out_specs=[vmem()] * 2,
        compiler_params=params(2),
        cost_estimate=cost(PACK_COST, 0),
        name="pack",
    )(*parts)


def cached_kernel(query_all, keys, values, accum, stats, query):
    extent, _, rows = query_all.shape
    for s in range(extent // SQ):
        for j in range(SQ):
            query[:, j * rows : (j + 1) * rows] = query_all[s * SQ + j]
        for h in range(HQ):
            head = slice(h * HEAD, (h + 1) * HEAD)
            score = jnp.dot(keys[h], query[head, :], preferred_element_type=f32)
            top = jnp.max(score, axis=0, keepdims=True)
            weights = jnp.exp(score - top)
            total = jnp.sum(weights, axis=0, keepdims=True)
            blended = jnp.dot(values[head, :], weights.astype(bf16), preferred_element_type=f32)
            accum[s, head, :] = blended
            stats[s, h : h + 1, :] = top
            stats[s, 8 + h : 9 + h, :] = total


def cached_call(queries, keys, values):
    extent, _, rows = queries.shape
    pairs = extent * rows * keys.shape[1] * HQ
    return pl.pallas_call(
        cached_kernel,
        out_shape=[
            jax.ShapeDtypeStruct((extent // SQ, QD, SQ * rows), f32),
            jax.ShapeDtypeStruct((extent // SQ, 16, SQ * rows), f32),
        ],
        in_specs=[vmem()] * 3,
        out_specs=[vmem()] * 2,
        scratch_shapes=[pltpu.VMEM((QD, SQ * rows), bf16)],
        compiler_params=params(12),
        cost_estimate=cost(CACHED_COST, 0, 0),
        name="attend_cached",
    )(queries, keys, values)


CACHED_COST = 1e9


def widen(part, lanes, width, fill):
    rows = part.shape[0]
    pieces = []
    if lanes.start:
        pieces.append(jnp.full((rows, lanes.start), fill, f32))
    pieces.append(part)
    if lanes.stop < width:
        pieces.append(jnp.full((rows, width - lanes.stop), fill, f32))
    return jnp.concatenate(pieces, axis=1)


def suffix_kernel(place, lengths, query_all, accum, stats, *rest):
    suffix, (w_hbm, outs, w_out, pairs, lse, sems) = rest[:SQ], rest[SQ:]
    copies = fetch([w_hbm], [w_out], sems)
    extent, _, rows = query_all.shape
    i = lax.rem(place[0], SQ)
    square = lax.div(place[0], SQ)
    width = SQ * rows
    for m in range(SQ):
        pairs[jnp.bitwise_xor(i, m)] = suffix[m][...]
    lse[...] = jnp.zeros_like(lse)
    for shift in range(extent // SQ):
        query_square = jnp.bitwise_xor(square, shift)
        position = query_square * width + lax.broadcasted_iota(jnp.int32, (1, width), 1)
        first = jnp.zeros((1, width), jnp.int32)
        bound = jnp.int32(0)
        for r in range(lengths.shape[1]):
            bound = bound + lengths[0, r]
            first = jnp.where(position >= bound, bound, first)
        windows = [(SQ - 2, 0, 1), (SQ - 1, 0, 2)]
        if not shift:
            windows = [(j, j, min(SQ, j + 3)) for j in range(SQ)]
        masks = []
        for block, begin, end in windows:
            lanes = slice(begin * rows, end * rows)
            key_at = (square * SQ + block) * rows + lax.broadcasted_iota(
                jnp.int32, (rows, lanes.stop - lanes.start), 0
            )
            masks.append((key_at >= first[:, lanes]) & (key_at <= position[:, lanes]))
        for h in range(HQ):
            head = slice(h * HEAD, (h + 1) * HEAD)
            head_v = slice(QD + h * HEAD, QD + (h + 1) * HEAD)
            query = [query_all[query_square * SQ + j, head, :] for j in range(windows[-1][2])]
            cached_top = stats[query_square, h : h + 1, :]
            top = cached_top
            pieces = []
            for (block, begin, end), mask in zip(windows, masks):
                lanes = slice(begin * rows, end * rows)
                score = jnp.dot(
                    pairs[block, head, :].T,
                    jnp.concatenate(query[begin:end], axis=1),
                    preferred_element_type=f32,
                )
                score = jnp.where(mask, score, NEG)
                level = jnp.max(score, axis=0, keepdims=True)
                top = jnp.maximum(top, widen(level, lanes, width, NEG))
                pieces.append((score, block, lanes))
            shrink = jnp.exp(cached_top - top)
            total = stats[query_square, 8 + h : 9 + h, :] * shrink
            mixed = accum[query_square, head, :] * shrink
            for score, block, lanes in pieces:
                weights = jnp.exp(score - top[:, lanes])
                total = total + widen(jnp.sum(weights, axis=0, keepdims=True), lanes, width, 0.0)
                blended = jnp.dot(
                    pairs[block, head_v, :], weights.astype(bf16), preferred_element_type=f32
                )
                mixed = mixed + widen(blended, lanes, width, 0.0)
            out = (mixed * (1.0 / total)).astype(bf16)
            for j in range(SQ):
                outs[query_square * SQ + j, head, :] = out[:, j * rows : (j + 1) * rows]
            level = top + jnp.log(total)
            high = level.astype(bf16).astype(f32)
            middle = (level - high).astype(bf16).astype(f32)
            for n, piece in enumerate((high, middle, level - high - middle)):
                lse[n * HQ + h : n * HQ + h + 1, :] = piece
        for j in range(SQ):
            outs[query_square * SQ + j, QD:, :] = lse[:, j * rows : (j + 1) * rows].astype(bf16)
    wait(copies)


def suffix_call(place, lengths, queries, accum, stats, suffix, w_out):
    extent, _, rows = queries.shape
    return pl.pallas_call(
        suffix_kernel,
        out_shape=[
            jax.ShapeDtypeStruct((extent, QD + LSE, rows), bf16),
            jax.ShapeDtypeStruct(w_out.shape, bf16),
        ],
        in_specs=[smem(), smem()] + [vmem()] * (3 + SQ) + [hbm()],
        out_specs=[vmem()] * 2,
        scratch_shapes=[
            pltpu.VMEM((SQ, 2 * QD, rows), bf16),
            pltpu.VMEM((LSE, SQ * rows), f32),
            pltpu.SemaphoreType.DMA((1,)),
        ],
        compiler_params=params(8),
        cost_estimate=cost(2e10, 8 * MIB, 0),
        name="attend_suffix",
    )(place, lengths, queries, accum, stats, *suffix, w_out)


def project_kernel(tokens_hbm, rate_hbm, w_out, parts, hidden_out, flat_out, mix, *rest):
    tokens, rate, sems = rest
    copies = fetch((tokens_hbm, rate_hbm), (tokens, rate), sems)
    squares = parts.shape[0] // SQ
    for j in range(SQ):
        group = [parts.at[s * SQ + j] for s in range(squares)]
        levels = []
        for part in group:
            pieces = part[QD:, :].astype(f32)
            levels.append(pieces[:HQ] + pieces[HQ : 2 * HQ] + pieces[2 * HQ : 3 * HQ])
        top = functools.reduce(jnp.maximum, levels)
        weights = [jnp.exp(v - top) for v in levels]
        inverse = 1.0 / functools.reduce(jnp.add, weights)
        weights = [w * inverse for w in weights]
        for h in range(HQ):
            head = slice(h * HEAD, (h + 1) * HEAD)
            mixed = functools.reduce(
                jnp.add, [w[h : h + 1, :] * p[head, :].astype(f32) for w, p in zip(weights, group)]
            )
            at = j * QD + h * HEAD
            mix[at : at + HEAD, :] = mixed.astype(bf16)
    wait(copies)
    hidden = unit(tokens[...].astype(f32))
    attn = jnp.concatenate(
        [mix[c * 128 : (c + 1) * 128, :].astype(f32).T.astype(bf16) for c in range(D // 128)], axis=1
    )
    attended = unit(jnp.dot(attn, w_out[...], preferred_element_type=f32))
    hidden = unit(hidden + over_rows(rate, hidden.shape[0]) * (attended - hidden))
    hidden_out[...] = hidden
    flat_out[...] = hidden.astype(bf16)


def project_call(tokens, rate, w_out, parts):
    rows = tokens.shape[0]
    return pl.pallas_call(
        project_kernel,
        out_shape=[jax.ShapeDtypeStruct((rows, D), f32), jax.ShapeDtypeStruct((rows, D), bf16)],
        in_specs=[hbm(), hbm(), vmem(), vmem()],
        out_specs=[vmem()] * 2,
        scratch_shapes=[pltpu.VMEM((D, rows), bf16)] + fetched(tokens, rate),
        compiler_params=params(8),
        cost_estimate=cost(2 * rows * D * D, D * D * 2),
        name="project",
    )(tokens, rate, w_out, parts)


def feed(first, second, w_up, w_gate, w_down, up_scale, gate_scale, keep, send):
    rows = first.shape[0]
    data = jnp.concatenate([first[...], second[...]], axis=0)
    up = jnp.dot(data, w_up(), preferred_element_type=f32) * over_rows(up_scale, 2 * rows)
    gate = jnp.dot(data, w_gate(), preferred_element_type=f32)
    gate = gate * (over_rows(gate_scale, 2 * rows) * math.sqrt(D))
    act = (up * (gate / (1.0 + jnp.exp(-gate)))).astype(bf16)
    part = jnp.dot(act, w_down(), preferred_element_type=f32)
    keep[...] = part[:rows, :]
    send[...] = part[rows:, :].astype(bf16)


def mlp_first_kernel(first, second, *rest):
    sources, (keep, send), held, sems = rest[:5], rest[5:7], rest[7:12], rest[12]
    copies = fetch(sources, held, sems)

    def ready(n):
        def get():
            copies[n].wait()
            return held[n][...]

        return get

    wait(copies[3:])
    feed(first, second, ready(0), ready(1), ready(2), held[3], held[4], keep, send)


def mlp_next_kernel(first, second, w_up, w_gate, w_down, up_scale, gate_scale, keep, send):
    feed(
        first,
        second,
        lambda: w_up[...],
        lambda: w_gate[...],
        lambda: w_down[...],
        up_scale,
        gate_scale,
        keep,
        send,
    )


def mlp_call(first, second, weights, held=False):
    rows = first.shape[0]
    units = weights[0].shape[1]
    out_shape = [jax.ShapeDtypeStruct((rows, D), f32), jax.ShapeDtypeStruct((rows, D), bf16)]
    if not held:
        out_shape += [jax.ShapeDtypeStruct(w.shape, w.dtype) for w in weights]
    return pl.pallas_call(
        mlp_next_kernel if held else mlp_first_kernel,
        out_shape=out_shape,
        in_specs=[vmem()] * 2 + [vmem() if held else hbm()] * 5,
        out_specs=[vmem()] * len(out_shape),
        scratch_shapes=[] if held else [pltpu.SemaphoreType.DMA((5,))],
        compiler_params=params(16),
        cost_estimate=cost(2 * 2 * rows * D * units * 3, 3 * D * units * 2, 2 * rows * units),
        name="mlp_held" if held else "mlp",
    )(first, second, *weights)


def add_kernel(kept, arrived, out):
    out[...] = (kept[...] + arrived[...].astype(f32)).astype(bf16)


def add_call(kept, arrived):
    return pl.pallas_call(
        add_kernel,
        out_shape=jax.ShapeDtypeStruct(kept.shape, bf16),
        in_specs=[vmem()] * 2,
        out_specs=vmem(),
        compiler_params=params(8),
        cost_estimate=cost(kept.size, kept.size * 8),
        name="add_partials",
    )(kept, arrived)


def final_kernel(hidden, rate_hbm, kept, *rest):
    arrived, (out, rate, sems) = rest[:-3], rest[-3:]
    copies = fetch([rate_hbm], [rate], sems)
    total = kept[...]
    for part in arrived:
        total = total + part[...].astype(f32)
    state = hidden[...]
    wait(copies)
    state = unit(state + over_rows(rate, state.shape[0]) * (unit(total) - state))
    out[...] = (math.sqrt(D) * state).astype(bf16)


def final_call(hidden, rate, kept, arrived):
    return pl.pallas_call(
        final_kernel,
        out_shape=jax.ShapeDtypeStruct(hidden.shape, bf16),
        in_specs=[vmem(), hbm()] + [vmem()] * (1 + len(arrived)),
        out_specs=pl.BlockSpec(hidden.shape, lambda: (0, 0)),
        scratch_shapes=fetched(rate),
        compiler_params=params(8),
        cost_estimate=cost(hidden.size * 10, hidden.size * 12),
        name="finish",
    )(hidden, rate, kept, *arrived)


def swap(shard, axis, mask):
    length = lax.axis_size(axis)
    return lax.ppermute(shard, axis, [(j, j ^ mask) for j in range(length)])


def body(
    tokens,
    seg_lengths,
    prefix_keys,
    prefix_values,
    w_qkv,
    w_out,
    qk_scale,
    attn_rate,
    w_up,
    w_gate,
    w_down,
    up_scale,
    gate_scale,
    mlp_rate,
):
    extent = lax.axis_size("tok")
    squares = extent // SQ
    place = lax.axis_index("tok").astype(jnp.int32).reshape(1)
    own = tokens[0]
    rows = own.shape[0]

    *cached, hidden, columns = prefix_call(
        place, qk_scale, prefix_keys[0], prefix_values[0], own
    )
    prefix = [cached[0]] + [swap(cached[m], "tok", m) for m in range(1, SQ)]
    queries, *sent = qkv_call(squares, place, hidden, columns, w_qkv)
    suffix = [sent[0]] + [swap(sent[m], "tok", m) for m in range(1, SQ)]
    queries = lax.all_to_all(queries.reshape(extent, QD, rows), "tok", 0, 0)
    accum, stats = cached_call(queries, *pack_call(prefix))
    parts, w_out = suffix_call(place, seg_lengths, queries, accum, stats, suffix, w_out)
    parts = lax.all_to_all(parts, "tok", 0, 0)
    hidden, flat = project_call(own, attn_rate, w_out, parts)

    weights = (w_up, w_gate, w_down, up_scale, gate_scale)
    chips = lax.axis_size("grp") // 2
    remote = [swap(flat, "grp", 2 * c) for c in range(1, chips)]
    keep, send, *weights = mlp_call(flat, swap(flat, "grp", 1), weights)
    arrived = [swap(send, "grp", 1)]
    for c in range(1, chips):
        data, keep = lax.optimization_barrier((remote[c - 1], keep))
        kept, send = mlp_call(data, swap(data, "grp", 1), weights, held=True)
        arrived.append(swap(add_call(kept, swap(send, "grp", 1)), "grp", 2 * c))
    return final_call(hidden, mlp_rate, keep, arrived)[None]


def solution(mesh):
    in_specs = (
        P("grp", "tok", None),
        P("grp", None),
        P("grp", "tok", None),
        P("grp", "tok", None),
        P(),
        P(),
        P(),
        P(),
        P(None, "grp"),
        P(None, "grp"),
        P("grp", None),
        P("grp"),
        P("grp"),
        P(),
    )
    out_specs = P("grp", "tok", None)
    return jax.shard_map(body, mesh=mesh, in_specs=in_specs, out_specs=out_specs, check_vma=False)
```

```python
import functools
import math

import jax
import jax.numpy as jnp
from jax import lax
from jax.experimental import pallas as pl
from jax.experimental.pallas import tpu as pltpu
from jax.sharding import PartitionSpec as P

D = 1280
HEADS = 20
HEAD = 64
EPS = 1e-06
SQ = 4
HQ = HEADS // SQ
QD = HQ * HEAD
LSE = 16
NEG = -1e30
PREFIX_LIMIT = 61
QKV_LIMIT = 50
MIB = 1 << 20

f32 = jnp.float32
bf16 = jnp.bfloat16


def unit(vector):
    return vector * lax.rsqrt(jnp.sum(vector * vector, axis=-1, keepdims=True) + EPS)


def head_unit_t(block, scale):
    dims, rows = block.shape
    per_head = block.reshape(dims // HEAD, HEAD, rows)
    total = jnp.sum(per_head * per_head, axis=1, keepdims=True)
    return (per_head * lax.rsqrt(total + EPS)).reshape(dims, rows) * scale


def params(limit):
    return pltpu.CompilerParams(vmem_limit_bytes=limit * MIB)


def vmem():
    return pl.BlockSpec(memory_space=pltpu.VMEM)


def hbm():
    return pl.BlockSpec(memory_space=pltpu.HBM)


def fetch(sources, targets, sems):
    copies = [
        pltpu.make_async_copy(a, b, sems.at[n]) for n, (a, b) in enumerate(zip(sources, targets))
    ]
    for copy in copies:
        copy.start()
    return copies


def wait(copies):
    for copy in copies:
        copy.wait()


def fetched(*arrays):
    return [pltpu.VMEM(a.shape, a.dtype) for a in arrays] + [
        pltpu.SemaphoreType.DMA((len(arrays),))
    ]


def over_rows(vector, rows):
    tiles = [
        jnp.broadcast_to(vector[c * 128 : (c + 1) * 128], (rows, 128))
        for c in range(vector.shape[0] // 128)
    ]
    return jnp.concatenate(tiles, axis=1)


def smem():
    return pl.BlockSpec(memory_space=pltpu.SMEM)


def cost(flops, nbytes, trans=0):
    return pl.CostEstimate(flops=int(flops), bytes_accessed=int(nbytes), transcendentals=int(trans))


def column(scale, c):
    return jnp.broadcast_to(scale[c * 128 : (c + 1) * 128], (128, 128)).T


def prefix_kernel(place, *rest):
    sources, outs, (parts, scale, keys, values, sems) = rest[:3], rest[3 : 3 + SQ], rest[3 + SQ :]
    copies = fetch(sources, (scale, keys, values), sems)
    rows = keys.shape[0]
    wait(copies[:2])
    for c in range(D // 128):
        cols = slice(c * 128, (c + 1) * 128)
        scale_t = jnp.concatenate([column(scale, c)] * (rows // 128), axis=1)
        split(parts, 0, c, head_unit_t(keys[:, cols].T.astype(f32), scale_t).astype(bf16))
    wait(copies[2:])
    for c in range(D // 128):
        split(parts, QD, c, values[:, c * 128 : (c + 1) * 128].T)
    i = lax.rem(place[0], SQ)
    for m in range(SQ):
        outs[m][...] = parts[jnp.bitwise_xor(i, m)]


def split(out, base, c, block):
    for part in range(0, 128, HEAD):
        row = c * 128 + part
        at = base + row % QD
        out[row // QD, at : at + HEAD, :] = block[part : part + HEAD, :]


def prefix_call(place, scale, keys, values):
    rows = keys.shape[0]
    return pl.pallas_call(
        prefix_kernel,
        out_shape=[jax.ShapeDtypeStruct((2 * QD, rows), bf16)] * SQ,
        in_specs=[smem()] + [hbm()] * 3,
        out_specs=[vmem()] * SQ,
        scratch_shapes=[pltpu.VMEM((SQ, 2 * QD, rows), bf16)] + fetched(scale, keys, values),
        compiler_params=params(PREFIX_LIMIT),
        cost_estimate=cost(5e10, 4 * rows * D * 2),
        name="prefix_prep",
    )(place, scale, keys, values)


def qkv_kernel(squares, place, tokens_hbm, scale_hbm, w_hbm, queries, *rest):
    outs, (parts, tokens, scale, sems, weights, w_sems) = rest[:SQ], rest[SQ:]
    small = fetch((tokens_hbm, scale_hbm), (tokens, scale), sems)
    spans = [pl.ds(p * D, D) for p in range(3)]
    copies = fetch([w_hbm.at[:, p] for p in spans], [weights.at[:, p] for p in spans], w_sems)
    wait(small)
    rows = tokens.shape[0]
    hidden = unit(tokens[...].astype(f32)).astype(bf16)
    columns = [column(scale, c)[:, :rows] for c in range(D // 128)]
    for part in range(3):
        copies[part].wait()
        out = jnp.dot(hidden, weights[:, part * D : (part + 1) * D], preferred_element_type=f32)
        for c in range(D // 128):
            block = out[:, c * 128 : (c + 1) * 128].T
            if part < 2:
                block = head_unit_t(block, columns[c])
            if part == 0:
                block = (block * math.sqrt(HEAD)).astype(bf16)
                for s in range(squares):
                    queries[s * D + c * 128 : s * D + (c + 1) * 128, :] = block
            else:
                split(parts, (part - 1) * QD, c, block.astype(bf16))
    i = lax.rem(place[0], SQ)
    for m in range(SQ):
        outs[m][...] = parts[jnp.bitwise_xor(i, m)]


def qkv_call(squares, place, tokens, scale, weights):
    rows = tokens.shape[0]
    pair = jax.ShapeDtypeStruct((2 * QD, rows), bf16)
    return pl.pallas_call(
        functools.partial(qkv_kernel, squares),
        out_shape=[jax.ShapeDtypeStruct((squares * D, rows), bf16)] + [pair] * SQ,
        in_specs=[smem()] + [hbm()] * 3,
        out_specs=[vmem()] * (1 + SQ),
        scratch_shapes=[
            pltpu.VMEM((SQ, 2 * QD, rows), bf16),
            *fetched(tokens, scale),
            pltpu.VMEM((D, 3 * D), bf16),
            pltpu.SemaphoreType.DMA((3,)),
        ],
        compiler_params=params(QKV_LIMIT),
        cost_estimate=cost(5e10, 3 * D * D * 2),
        name="qkv",
    )(place, tokens, scale, weights)


def arrive_kernel(*refs):
    parts, out = refs[:-1], refs[-1]
    out[...] = functools.reduce(jnp.add, [p[:16, :128].astype(f32) for p in parts])


ARRIVE_COST = 20e9


def arrive_call(parts):
    return pl.pallas_call(
        arrive_kernel,
        out_shape=jax.ShapeDtypeStruct((16, 128), f32),
        in_specs=[vmem()] * len(parts),
        out_specs=vmem(),
        compiler_params=params(2),
        cost_estimate=cost(ARRIVE_COST, 0),
        name="arrive",
    )(*parts)


def cached_kernel(query_all, _, *rest):
    prefix, (accum, stats, query, keys, values) = rest[:SQ], rest[SQ:]
    extent, _, rows = query_all.shape
    span = prefix[0].shape[1]
    for n, part in enumerate(prefix):
        at = slice(n * span, (n + 1) * span)
        for h in range(HQ):
            keys[h, at, :] = part[h * HEAD : (h + 1) * HEAD, :].T
        values[:, at] = part[QD:, :]
    for s in range(extent // SQ):
        for j in range(SQ):
            query[:, j * rows : (j + 1) * rows] = query_all[s * SQ + j]
        for h in range(HQ):
            head = slice(h * HEAD, (h + 1) * HEAD)
            score = jnp.dot(keys[h], query[head, :], preferred_element_type=f32)
            top = jnp.max(score, axis=0, keepdims=True)
            weights = jnp.exp(score - top)
            total = jnp.sum(weights, axis=0, keepdims=True)
            blended = jnp.dot(values[head, :], weights.astype(bf16), preferred_element_type=f32)
            accum[s, head, :] = blended
            stats[s, h : h + 1, :] = top
            stats[s, 8 + h : 9 + h, :] = total


def cached_call(queries, arrived, prefix):
    extent, _, rows = queries.shape
    span = prefix[0].shape[1]
    return pl.pallas_call(
        cached_kernel,
        out_shape=[
            jax.ShapeDtypeStruct((extent // SQ, QD, SQ * rows), f32),
            jax.ShapeDtypeStruct((extent // SQ, 16, SQ * rows), f32),
        ],
        in_specs=[vmem()] * (2 + SQ),
        out_specs=[vmem()] * 2,
        scratch_shapes=[
            pltpu.VMEM((QD, SQ * rows), bf16),
            pltpu.VMEM((HQ, SQ * span, HEAD), bf16),
            pltpu.VMEM((QD, SQ * span), bf16),
        ],
        compiler_params=params(12),
        cost_estimate=cost(CACHED_COST, 0, 0),
        name="attend_cached",
    )(queries, arrived, *prefix)


CACHED_COST = 1e9


def widen(part, lanes, width, fill):
    rows = part.shape[0]
    pieces = []
    if lanes.start:
        pieces.append(jnp.full((rows, lanes.start), fill, f32))
    pieces.append(part)
    if lanes.stop < width:
        pieces.append(jnp.full((rows, width - lanes.stop), fill, f32))
    return jnp.concatenate(pieces, axis=1)


def suffix_kernel(place, lengths, query_all, accum, stats, *rest):
    suffix, (w_hbm, outs, w_out, pairs, lse, sems) = rest[:SQ], rest[SQ:]
    copies = fetch([w_hbm], [w_out], sems)
    extent, _, rows = query_all.shape
    i = lax.rem(place[0], SQ)
    square = lax.div(place[0], SQ)
    width = SQ * rows
    for m in range(SQ):
        pairs[jnp.bitwise_xor(i, m)] = suffix[m][...]
    lse[...] = jnp.zeros_like(lse)
    for shift in range(extent // SQ):
        query_square = jnp.bitwise_xor(square, shift)
        position = query_square * width + lax.broadcasted_iota(jnp.int32, (1, width), 1)
        first = jnp.zeros((1, width), jnp.int32)
        bound = jnp.int32(0)
        for r in range(lengths.shape[1]):
            bound = bound + lengths[0, r]
            first = jnp.where(position >= bound, bound, first)
        windows = [(SQ - 2, 0, 1), (SQ - 1, 0, 2)]
        if not shift:
            windows = [(j, j, min(SQ, j + 3)) for j in range(SQ)]
        masks = []
        for block, begin, end in windows:
            lanes = slice(begin * rows, end * rows)
            key_at = (square * SQ + block) * rows + lax.broadcasted_iota(
                jnp.int32, (rows, lanes.stop - lanes.start), 0
            )
            masks.append((key_at >= first[:, lanes]) & (key_at <= position[:, lanes]))
        scores = []
        for h in range(HQ):
            head = slice(h * HEAD, (h + 1) * HEAD)
            query = [query_all[query_square * SQ + j, head, :] for j in range(windows[-1][2])]
            for (block, begin, end), mask in zip(windows, masks):
                score = jnp.dot(
                    pairs[block, head, :].T,
                    jnp.concatenate(query[begin:end], axis=1),
                    preferred_element_type=f32,
                )
                scores.append(jnp.where(mask, score, NEG))
        states = []
        for h in range(HQ):
            cached_top = stats[query_square, h : h + 1, :]
            top = cached_top
            part = scores[h * len(windows) : (h + 1) * len(windows)]
            for score, (block, begin, end) in zip(part, windows):
                lanes = slice(begin * rows, end * rows)
                level = jnp.max(score, axis=0, keepdims=True)
                top = jnp.maximum(top, widen(level, lanes, width, NEG))
            shrink = jnp.exp(cached_top - top)
            total = stats[query_square, 8 + h : 9 + h, :] * shrink
            weights = []
            for score, (block, begin, end) in zip(part, windows):
                lanes = slice(begin * rows, end * rows)
                weight = jnp.exp(score - top[:, lanes])
                total = total + widen(jnp.sum(weight, axis=0, keepdims=True), lanes, width, 0.0)
                weights.append(weight.astype(bf16))
            states.append((top, shrink, total, weights))
        for h, (top, shrink, total, weights) in enumerate(states):
            head = slice(h * HEAD, (h + 1) * HEAD)
            head_v = slice(QD + h * HEAD, QD + (h + 1) * HEAD)
            mixed = accum[query_square, head, :] * shrink
            for weight, (block, begin, end) in zip(weights, windows):
                lanes = slice(begin * rows, end * rows)
                blended = jnp.dot(pairs[block, head_v, :], weight, preferred_element_type=f32)
                mixed = mixed + widen(blended, lanes, width, 0.0)
            out = (mixed * (1.0 / total)).astype(bf16)
            for j in range(SQ):
                outs[query_square * SQ + j, head, :] = out[:, j * rows : (j + 1) * rows]
            level = top + jnp.log(total)
            high = level.astype(bf16).astype(f32)
            middle = (level - high).astype(bf16).astype(f32)
            for n, piece in enumerate((high, middle, level - high - middle)):
                lse[n * HQ + h : n * HQ + h + 1, :] = piece
        for j in range(SQ):
            outs[query_square * SQ + j, QD:, :] = lse[:, j * rows : (j + 1) * rows].astype(bf16)
    wait(copies)


def suffix_call(place, lengths, queries, accum, stats, suffix, w_out):
    extent, _, rows = queries.shape
    return pl.pallas_call(
        suffix_kernel,
        out_shape=[
            jax.ShapeDtypeStruct((extent, QD + LSE, rows), bf16),
            jax.ShapeDtypeStruct(w_out.shape, bf16),
        ],
        in_specs=[smem(), smem()] + [vmem()] * (3 + SQ) + [hbm()],
        out_specs=[vmem()] * 2,
        scratch_shapes=[
            pltpu.VMEM((SQ, 2 * QD, rows), bf16),
            pltpu.VMEM((LSE, SQ * rows), f32),
            pltpu.SemaphoreType.DMA((1,)),
        ],
        compiler_params=params(8),
        cost_estimate=cost(2e10, 8 * MIB, 0),
        name="attend_suffix",
    )(place, lengths, queries, accum, stats, *suffix, w_out)


def project_kernel(tokens_hbm, rate_hbm, w_out, parts, hidden_out, flat_out, mix, *rest):
    tokens, rate, sems = rest
    copies = fetch((tokens_hbm, rate_hbm), (tokens, rate), sems)
    squares = parts.shape[0] // SQ
    for j in range(SQ):
        group = [parts.at[s * SQ + j] for s in range(squares)]
        levels = []
        for part in group:
            pieces = part[QD:, :].astype(f32)
            levels.append(pieces[:HQ] + pieces[HQ : 2 * HQ] + pieces[2 * HQ : 3 * HQ])
        top = functools.reduce(jnp.maximum, levels)
        weights = [jnp.exp(v - top) for v in levels]
        inverse = 1.0 / functools.reduce(jnp.add, weights)
        weights = [w * inverse for w in weights]
        for h in range(HQ):
            head = slice(h * HEAD, (h + 1) * HEAD)
            mixed = functools.reduce(
                jnp.add, [w[h : h + 1, :] * p[head, :].astype(f32) for w, p in zip(weights, group)]
            )
            at = j * QD + h * HEAD
            mix[at : at + HEAD, :] = mixed.astype(bf16)
    wait(copies)
    hidden = unit(tokens[...].astype(f32))
    attn = jnp.concatenate(
        [mix[c * 128 : (c + 1) * 128, :].astype(f32).T.astype(bf16) for c in range(D // 128)], axis=1
    )
    attended = unit(jnp.dot(attn, w_out[...], preferred_element_type=f32))
    hidden = unit(hidden + over_rows(rate, hidden.shape[0]) * (attended - hidden))
    hidden_out[...] = hidden
    flat_out[...] = hidden.astype(bf16)


def project_call(tokens, rate, w_out, parts):
    rows = tokens.shape[0]
    return pl.pallas_call(
        project_kernel,
        out_shape=[jax.ShapeDtypeStruct((rows, D), f32), jax.ShapeDtypeStruct((rows, D), bf16)],
        in_specs=[hbm(), hbm(), vmem(), vmem()],
        out_specs=[vmem()] * 2,
        scratch_shapes=[pltpu.VMEM((D, rows), bf16)] + fetched(tokens, rate),
        compiler_params=params(8),
        cost_estimate=cost(2 * rows * D * D, D * D * 2),
        name="project",
    )(tokens, rate, w_out, parts)


def mlp_kernel(first, second, w_up, w_gate, w_down, up_scale, gate_scale, keep, send):
    rows = first.shape[0]
    data = jnp.concatenate([first[...], second[...]], axis=0)
    up = jnp.dot(data, w_up[...], preferred_element_type=f32) * over_rows(up_scale, 2 * rows)
    gate = jnp.dot(data, w_gate[...], preferred_element_type=f32)
    gate = gate * (over_rows(gate_scale, 2 * rows) * math.sqrt(D))
    act = (up * (gate / (1.0 + jnp.exp(-gate)))).astype(bf16)
    part = jnp.dot(act, w_down[...], preferred_element_type=f32)
    keep[...] = part[:rows, :]
    send[...] = part[rows:, :].astype(bf16)


def mlp_call(first, second, weights):
    rows = first.shape[0]
    units = weights[0].shape[1]
    return pl.pallas_call(
        mlp_kernel,
        out_shape=[jax.ShapeDtypeStruct((rows, D), f32), jax.ShapeDtypeStruct((rows, D), bf16)],
        in_specs=[vmem()] * 7,
        out_specs=[vmem()] * 2,
        compiler_params=params(12),
        cost_estimate=cost(2 * 2 * rows * D * units * 3, 3 * D * units * 2, 2 * rows * units),
        name="mlp",
    )(first, second, *weights)


def add_kernel(kept, arrived, out):
    out[...] = (kept[...] + arrived[...].astype(f32)).astype(bf16)


def add_call(kept, arrived):
    return pl.pallas_call(
        add_kernel,
        out_shape=jax.ShapeDtypeStruct(kept.shape, bf16),
        in_specs=[vmem()] * 2,
        out_specs=vmem(),
        compiler_params=params(8),
        cost_estimate=cost(kept.size, kept.size * 8),
        name="add_partials",
    )(kept, arrived)


def final_kernel(hidden, rate_hbm, kept, *rest):
    arrived, (out, rate, sems) = rest[:-3], rest[-3:]
    copies = fetch([rate_hbm], [rate], sems)
    total = kept[...]
    for part in arrived:
        total = total + part[...].astype(f32)
    state = hidden[...]
    wait(copies)
    state = unit(state + over_rows(rate, state.shape[0]) * (unit(total) - state))
    out[...] = (math.sqrt(D) * state).astype(bf16)


def final_call(hidden, rate, kept, arrived):
    return pl.pallas_call(
        final_kernel,
        out_shape=jax.ShapeDtypeStruct(hidden.shape, bf16),
        in_specs=[vmem(), hbm()] + [vmem()] * (1 + len(arrived)),
        out_specs=pl.BlockSpec(hidden.shape, lambda: (0, 0)),
        scratch_shapes=fetched(rate),
        compiler_params=params(8),
        cost_estimate=cost(hidden.size * 10, hidden.size * 12),
        name="finish",
    )(hidden, rate, kept, *arrived)


def swap(shard, axis, mask):
    length = lax.axis_size(axis)
    return lax.ppermute(shard, axis, [(j, j ^ mask) for j in range(length)])


def body(
    tokens,
    seg_lengths,
    prefix_keys,
    prefix_values,
    w_qkv,
    w_out,
    qk_scale,
    attn_rate,
    w_up,
    w_gate,
    w_down,
    up_scale,
    gate_scale,
    mlp_rate,
):
    extent = lax.axis_size("tok")
    squares = extent // SQ
    place = lax.axis_index("tok").astype(jnp.int32).reshape(1)
    own = tokens[0]
    rows = own.shape[0]

    cached = prefix_call(place, qk_scale, prefix_keys[0], prefix_values[0])
    prefix = [cached[0]] + [swap(cached[m], "tok", m) for m in range(1, SQ)]
    queries, *sent = qkv_call(squares, place, own, qk_scale, w_qkv)
    suffix = [sent[0]] + [swap(sent[m], "tok", m) for m in range(1, SQ)]
    queries = lax.all_to_all(queries.reshape(extent, QD, rows), "tok", 0, 0)
    accum, stats = cached_call(queries, arrive_call(prefix), prefix)
    parts, w_out = suffix_call(place, seg_lengths, queries, accum, stats, suffix, w_out)
    parts = lax.all_to_all(parts, "tok", 0, 0)
    hidden, flat = project_call(own, attn_rate, w_out, parts)

    weights = (w_up, w_gate, w_down, up_scale, gate_scale)
    chips = lax.axis_size("grp") // 2
    remote = [swap(flat, "grp", 2 * c) for c in range(1, chips)]
    keep, send = mlp_call(flat, swap(flat, "grp", 1), weights)
    arrived = [swap(send, "grp", 1)]
    for c in range(1, chips):
        data, keep = lax.optimization_barrier((remote[c - 1], keep))
        kept, send = mlp_call(data, swap(data, "grp", 1), weights)
        arrived.append(swap(add_call(kept, swap(send, "grp", 1)), "grp", 2 * c))
    return final_call(hidden, mlp_rate, keep, arrived)[None]


def solution(mesh):
    in_specs = (
        P("grp", "tok", None),
        P("grp", None),
        P("grp", "tok", None),
        P("grp", "tok", None),
        P(),
        P(),
        P(),
        P(),
        P(None, "grp"),
        P(None, "grp"),
        P("grp", None),
        P("grp"),
        P("grp"),
        P(),
    )
    out_specs = P("grp", "tok", None)
    return jax.shard_map(body, mesh=mesh, in_specs=in_specs, out_specs=out_specs, check_vma=False)
```

```python
import functools
import math

import jax
import jax.numpy as jnp
from jax import lax
from jax.experimental import pallas as pl
from jax.experimental.pallas import tpu as pltpu
from jax.sharding import PartitionSpec as P

D = 1280
HEADS = 20
HEAD = 64
EPS = 1e-06
SQ = 4
HQ = HEADS // SQ
QD = HQ * HEAD
LSE = 16
NEG = -1e30
PREFIX_LIMIT = 61
QKV_LIMIT = 50
MIB = 1 << 20

f32 = jnp.float32
bf16 = jnp.bfloat16


def unit(vector):
    return vector * lax.rsqrt(jnp.sum(vector * vector, axis=-1, keepdims=True) + EPS)


def head_unit_t(block, scale):
    dims, rows = block.shape
    per_head = block.reshape(dims // HEAD, HEAD, rows)
    total = jnp.sum(per_head * per_head, axis=1, keepdims=True)
    return (per_head * lax.rsqrt(total + EPS)).reshape(dims, rows) * scale


def params(limit):
    return pltpu.CompilerParams(vmem_limit_bytes=limit * MIB)


def vmem():
    return pl.BlockSpec(memory_space=pltpu.VMEM)


def hbm():
    return pl.BlockSpec(memory_space=pltpu.HBM)


def fetch(sources, targets, sems):
    copies = [
        pltpu.make_async_copy(a, b, sems.at[n]) for n, (a, b) in enumerate(zip(sources, targets))
    ]
    for copy in copies:
        copy.start()
    return copies


def wait(copies):
    for copy in copies:
        copy.wait()


def fetched(*arrays):
    return [pltpu.VMEM(a.shape, a.dtype) for a in arrays] + [
        pltpu.SemaphoreType.DMA((len(arrays),))
    ]


def over_rows(vector, rows):
    tiles = [
        jnp.broadcast_to(vector[c * 128 : (c + 1) * 128], (rows, 128))
        for c in range(vector.shape[0] // 128)
    ]
    return jnp.concatenate(tiles, axis=1)


def smem():
    return pl.BlockSpec(memory_space=pltpu.SMEM)


def cost(flops, nbytes, trans=0):
    return pl.CostEstimate(flops=int(flops), bytes_accessed=int(nbytes), transcendentals=int(trans))


def column(scale, c):
    return jnp.broadcast_to(scale[c * 128 : (c + 1) * 128], (128, 128)).T


def prefix_kernel(place, *rest):
    sources, outs, (parts, scale, keys, values, sems) = rest[:3], rest[3 : 3 + SQ], rest[3 + SQ :]
    copies = fetch(sources, (scale, keys, values), sems)
    rows = keys.shape[0]
    wait(copies[:2])
    for c in range(D // 128):
        cols = slice(c * 128, (c + 1) * 128)
        scale_t = jnp.concatenate([column(scale, c)] * (rows // 128), axis=1)
        split(parts, 0, c, head_unit_t(keys[:, cols].T.astype(f32), scale_t).astype(bf16))
    wait(copies[2:])
    for c in range(D // 128):
        split(parts, QD, c, values[:, c * 128 : (c + 1) * 128].T)
    i = lax.rem(place[0], SQ)
    for m in range(SQ):
        outs[m][...] = parts[jnp.bitwise_xor(i, m)]


def split(out, base, c, block):
    for part in range(0, 128, HEAD):
        row = c * 128 + part
        at = base + row % QD
        out[row // QD, at : at + HEAD, :] = block[part : part + HEAD, :]


def prefix_call(place, scale, keys, values):
    rows = keys.shape[0]
    return pl.pallas_call(
        prefix_kernel,
        out_shape=[jax.ShapeDtypeStruct((2 * QD, rows), bf16)] * SQ,
        in_specs=[smem()] + [hbm()] * 3,
        out_specs=[vmem()] * SQ,
        scratch_shapes=[pltpu.VMEM((SQ, 2 * QD, rows), bf16)] + fetched(scale, keys, values),
        compiler_params=params(PREFIX_LIMIT),
        cost_estimate=cost(5e10, 4 * rows * D * 2),
        name="prefix_prep",
    )(place, scale, keys, values)


def qkv_kernel(squares, place, tokens_hbm, scale_hbm, w_hbm, queries, *rest):
    outs, (parts, tokens, scale, sems, weights, w_sems) = rest[:SQ], rest[SQ:]
    small = fetch((tokens_hbm, scale_hbm), (tokens, scale), sems)
    spans = [pl.ds(p * D, D) for p in range(3)]
    copies = fetch([w_hbm.at[:, p] for p in spans], [weights.at[:, p] for p in spans], w_sems)
    wait(small)
    rows = tokens.shape[0]
    hidden = unit(tokens[...].astype(f32)).astype(bf16)
    columns = [column(scale, c)[:, :rows] for c in range(D // 128)]
    for part in range(3):
        copies[part].wait()
        out = jnp.dot(hidden, weights[:, part * D : (part + 1) * D], preferred_element_type=f32)
        for c in range(D // 128):
            block = out[:, c * 128 : (c + 1) * 128].T
            if part < 2:
                block = head_unit_t(block, columns[c])
            if part == 0:
                block = (block * math.sqrt(HEAD)).astype(bf16)
                for s in range(squares):
                    queries[s * D + c * 128 : s * D + (c + 1) * 128, :] = block
            else:
                split(parts, (part - 1) * QD, c, block.astype(bf16))
    i = lax.rem(place[0], SQ)
    for m in range(SQ):
        outs[m][...] = parts[jnp.bitwise_xor(i, m)]


def qkv_call(squares, place, tokens, scale, weights):
    rows = tokens.shape[0]
    pair = jax.ShapeDtypeStruct((2 * QD, rows), bf16)
    return pl.pallas_call(
        functools.partial(qkv_kernel, squares),
        out_shape=[jax.ShapeDtypeStruct((squares * D, rows), bf16)] + [pair] * SQ,
        in_specs=[smem()] + [hbm()] * 3,
        out_specs=[vmem()] * (1 + SQ),
        scratch_shapes=[
            pltpu.VMEM((SQ, 2 * QD, rows), bf16),
            *fetched(tokens, scale),
            pltpu.VMEM((D, 3 * D), bf16),
            pltpu.SemaphoreType.DMA((3,)),
        ],
        compiler_params=params(QKV_LIMIT),
        cost_estimate=cost(5e10, 3 * D * D * 2),
        name="qkv",
    )(place, tokens, scale, weights)


def arrive_kernel(*refs):
    parts, out = refs[:-1], refs[-1]
    out[...] = functools.reduce(jnp.add, [p[:16, :128].astype(f32) for p in parts])


ARRIVE_COST = 20e9


def arrive_call(parts):
    return pl.pallas_call(
        arrive_kernel,
        out_shape=jax.ShapeDtypeStruct((16, 128), f32),
        in_specs=[vmem()] * len(parts),
        out_specs=vmem(),
        compiler_params=params(2),
        cost_estimate=cost(ARRIVE_COST, 0),
        name="arrive",
    )(*parts)


def cached_kernel(query_all, _, *rest):
    prefix, (accum, stats, keys, values) = rest[:SQ], rest[SQ:]
    extent, _, rows = query_all.shape
    span = prefix[0].shape[1]
    for n, part in enumerate(prefix):
        at = slice(n * span, (n + 1) * span)
        for h in range(HQ):
            keys[h, at, :] = part[h * HEAD : (h + 1) * HEAD, :].T
        values[:, at] = part[QD:, :]
    steps = [(s, h) for s in range(extent // SQ) for h in range(HQ)]
    cuts = [slice(k, k + 2 * span) for k in range(0, SQ * span, 2 * span)]

    def queries(s, h):
        head = slice(h * HEAD, (h + 1) * HEAD)
        return jnp.concatenate([query_all[s * SQ + j, head, :] for j in range(SQ)], axis=1)

    def part_scores(h, cut, query):
        return jnp.dot(keys[h, cut, :], query, preferred_element_type=f32)

    query = queries(0, 0)
    scores = [part_scores(0, cut, query) for cut in cuts]
    for n, (s, h) in enumerate(steps):
        head = slice(h * HEAD, (h + 1) * HEAD)
        top = functools.reduce(jnp.maximum, [jnp.max(x, axis=0, keepdims=True) for x in scores])
        following = steps[n + 1] if n + 1 < len(steps) else None
        if following:
            query = queries(*following)
        ahead, total, blended = [], 0.0, 0.0
        for cut, score in zip(cuts, scores):
            if following:
                ahead.append(part_scores(following[1], cut, query))
            weights = jnp.exp(score - top)
            total = total + jnp.sum(weights, axis=0, keepdims=True)
            blended = blended + jnp.dot(
                values[head, cut], weights.astype(bf16), preferred_element_type=f32
            )
        accum[s, head, :] = blended
        stats[s, h : h + 1, :] = top
        stats[s, 8 + h : 9 + h, :] = total
        scores = ahead


def cached_call(queries, arrived, prefix):
    extent, _, rows = queries.shape
    span = prefix[0].shape[1]
    return pl.pallas_call(
        cached_kernel,
        out_shape=[
            jax.ShapeDtypeStruct((extent // SQ, QD, SQ * rows), f32),
            jax.ShapeDtypeStruct((extent // SQ, 16, SQ * rows), f32),
        ],
        in_specs=[vmem()] * (2 + SQ),
        out_specs=[vmem()] * 2,
        scratch_shapes=[
            pltpu.VMEM((HQ, SQ * span, HEAD), bf16),
            pltpu.VMEM((QD, SQ * span), bf16),
        ],
        compiler_params=params(16),
        cost_estimate=cost(CACHED_COST, 0, 0),
        name="attend_cached",
    )(queries, arrived, *prefix)


CACHED_COST = 1e9


def widen(part, lanes, width, fill):
    rows = part.shape[0]
    pieces = []
    if lanes.start:
        pieces.append(jnp.full((rows, lanes.start), fill, f32))
    pieces.append(part)
    if lanes.stop < width:
        pieces.append(jnp.full((rows, width - lanes.stop), fill, f32))
    return jnp.concatenate(pieces, axis=1)


def suffix_kernel(count, place, lengths, query_all, accum, stats, *rest):
    suffix, w_hbm, rest = rest[:SQ], rest[SQ], rest[SQ + 1 :]
    outs, (w_out, pairs, mixes, sems) = rest[:count], rest[count:]
    copies = fetch([w_hbm], [w_out], sems)
    extent, _, rows = query_all.shape
    i = lax.rem(place[0], SQ)
    square = lax.div(place[0], SQ)
    width = SQ * rows
    for m in range(SQ):
        pairs[jnp.bitwise_xor(i, m)] = suffix[m][...]
    for shift in range(extent // SQ):
        query_square = jnp.bitwise_xor(square, shift)
        position = query_square * width + lax.broadcasted_iota(jnp.int32, (1, width), 1)
        first = jnp.zeros((1, width), jnp.int32)
        bound = jnp.int32(0)
        for r in range(lengths.shape[1]):
            bound = bound + lengths[0, r]
            first = jnp.where(position >= bound, bound, first)
        windows = [(SQ - 2, 0, 1), (SQ - 1, 0, 2)]
        if not shift:
            windows = [(j, j, min(SQ, j + 3)) for j in range(SQ)]
        masks = []
        for block, begin, end in windows:
            lanes = slice(begin * rows, end * rows)
            key_at = (square * SQ + block) * rows + lax.broadcasted_iota(
                jnp.int32, (rows, lanes.stop - lanes.start), 0
            )
            masks.append((key_at >= first[:, lanes]) & (key_at <= position[:, lanes]))
        scores = []
        for h in range(HQ):
            head = slice(h * HEAD, (h + 1) * HEAD)
            query = [query_all[query_square * SQ + j, head, :] for j in range(windows[-1][2])]
            for (block, begin, end), mask in zip(windows, masks):
                score = jnp.dot(
                    pairs[block, head, :].T,
                    jnp.concatenate(query[begin:end], axis=1),
                    preferred_element_type=f32,
                )
                scores.append(jnp.where(mask, score, NEG))
        states = []
        for h in range(HQ):
            cached_top = stats[query_square, h : h + 1, :]
            top = cached_top
            part = scores[h * len(windows) : (h + 1) * len(windows)]
            for score, (block, begin, end) in zip(part, windows):
                lanes = slice(begin * rows, end * rows)
                level = jnp.max(score, axis=0, keepdims=True)
                top = jnp.maximum(top, widen(level, lanes, width, NEG))
            shrink = jnp.exp(cached_top - top)
            total = stats[query_square, 8 + h : 9 + h, :] * shrink
            weights = []
            for score, (block, begin, end) in zip(part, windows):
                lanes = slice(begin * rows, end * rows)
                weight = jnp.exp(score - top[:, lanes])
                total = total + widen(jnp.sum(weight, axis=0, keepdims=True), lanes, width, 0.0)
                weights.append(weight.astype(bf16))
            states.append((top, shrink, total, weights))
        for h, (top, shrink, total, weights) in enumerate(states):
            head = slice(h * HEAD, (h + 1) * HEAD)
            head_v = slice(QD + h * HEAD, QD + (h + 1) * HEAD)
            mixed = accum[query_square, head, :] * shrink
            for weight, (block, begin, end) in zip(weights, windows):
                lanes = slice(begin * rows, end * rows)
                blended = jnp.dot(pairs[block, head_v, :], weight, preferred_element_type=f32)
                mixed = mixed + widen(blended, lanes, width, 0.0)
            mixes[head, :] = mixed * (1.0 / total)
            level = top + jnp.log(total)
            high = level.astype(bf16).astype(f32)
            middle = (level - high).astype(bf16).astype(f32)
            for n, piece in enumerate((high, middle, level - high - middle)):
                row = QD + n * HQ + h
                mixes[row : row + 1, :] = piece
        mixes[QD + LSE - 1 :, :] = jnp.zeros((1, width), f32)
        for m in range(SQ):
            lanes = pl.ds(pl.multiple_of(jnp.bitwise_xor(i, m) * rows, rows), rows)
            outs[shift * SQ + m][...] = mixes[:, lanes].astype(bf16)
    wait(copies)


def suffix_call(place, lengths, queries, accum, stats, suffix, w_out):
    extent, _, rows = queries.shape
    return pl.pallas_call(
        functools.partial(suffix_kernel, extent),
        out_shape=[jax.ShapeDtypeStruct((QD + LSE, rows), bf16)] * extent
        + [jax.ShapeDtypeStruct(w_out.shape, bf16)],
        in_specs=[smem(), smem()] + [vmem()] * (3 + SQ) + [hbm()],
        out_specs=[vmem()] * (extent + 1),
        scratch_shapes=[
            pltpu.VMEM((SQ, 2 * QD, rows), bf16),
            pltpu.VMEM((QD + LSE, SQ * rows), f32),
            pltpu.SemaphoreType.DMA((1,)),
        ],
        compiler_params=params(8),
        cost_estimate=cost(2e10, 8 * MIB, 0),
        name="attend_suffix",
    )(place, lengths, queries, accum, stats, *suffix, w_out)


def project_kernel(count, place, tokens_hbm, rate_hbm, w_out, *rest):
    arrived, rest = rest[:count], rest[count:]
    hidden_out, flat_out, mix, parts, tokens, rate, sems = rest
    copies = fetch((tokens_hbm, rate_hbm), (tokens, rate), sems)
    squares = count // SQ
    i = lax.rem(place[0], SQ)
    for m, part in enumerate(arrived):
        parts[m // SQ * SQ + jnp.bitwise_xor(i, m % SQ)] = part[...]
    for j in range(SQ):
        group = [parts.at[s * SQ + j] for s in range(squares)]
        levels = []
        for part in group:
            pieces = part[QD:, :].astype(f32)
            levels.append(pieces[:HQ] + pieces[HQ : 2 * HQ] + pieces[2 * HQ : 3 * HQ])
        top = functools.reduce(jnp.maximum, levels)
        weights = [jnp.exp(v - top) for v in levels]
        inverse = 1.0 / functools.reduce(jnp.add, weights)
        weights = [w * inverse for w in weights]
        for h in range(HQ):
            head = slice(h * HEAD, (h + 1) * HEAD)
            mixed = functools.reduce(
                jnp.add, [w[h : h + 1, :] * p[head, :].astype(f32) for w, p in zip(weights, group)]
            )
            at = j * QD + h * HEAD
            mix[at : at + HEAD, :] = mixed.astype(bf16)
    wait(copies)
    hidden = unit(tokens[...].astype(f32))
    attn = jnp.concatenate(
        [mix[c * 128 : (c + 1) * 128, :].astype(f32).T.astype(bf16) for c in range(D // 128)], axis=1
    )
    attended = unit(jnp.dot(attn, w_out[...], preferred_element_type=f32))
    hidden = unit(hidden + over_rows(rate, hidden.shape[0]) * (attended - hidden))
    hidden_out[...] = hidden
    flat_out[...] = hidden.astype(bf16)


def project_call(place, tokens, rate, w_out, parts):
    rows = tokens.shape[0]
    return pl.pallas_call(
        functools.partial(project_kernel, len(parts)),
        out_shape=[jax.ShapeDtypeStruct((rows, D), f32), jax.ShapeDtypeStruct((rows, D), bf16)],
        in_specs=[smem(), hbm(), hbm()] + [vmem()] * (1 + len(parts)),
        out_specs=[vmem()] * 2,
        scratch_shapes=[
            pltpu.VMEM((D, rows), bf16),
            pltpu.VMEM((len(parts), *parts[0].shape), bf16),
            *fetched(tokens, rate),
        ],
        compiler_params=params(8),
        cost_estimate=cost(2 * rows * D * D, D * D * 2),
        name="project",
    )(place, tokens, rate, w_out, *parts)


def mlp_kernel(first, second, w_up, w_gate, w_down, up_scale, gate_scale, keep, send):
    rows = first.shape[0]
    data = jnp.concatenate([first[...], second[...]], axis=0)
    up = jnp.dot(data, w_up[...], preferred_element_type=f32) * over_rows(up_scale, 2 * rows)
    gate = jnp.dot(data, w_gate[...], preferred_element_type=f32)
    gate = gate * (over_rows(gate_scale, 2 * rows) * math.sqrt(D))
    act = (up * (gate / (1.0 + jnp.exp(-gate)))).astype(bf16)
    part = jnp.dot(act, w_down[...], preferred_element_type=f32)
    keep[...] = part[:rows, :]
    send[...] = part[rows:, :].astype(bf16)


def mlp_call(first, second, weights):
    rows = first.shape[0]
    units = weights[0].shape[1]
    return pl.pallas_call(
        mlp_kernel,
        out_shape=[jax.ShapeDtypeStruct((rows, D), f32), jax.ShapeDtypeStruct((rows, D), bf16)],
        in_specs=[vmem()] * 7,
        out_specs=[vmem()] * 2,
        compiler_params=params(12),
        cost_estimate=cost(2 * 2 * rows * D * units * 3, 3 * D * units * 2, 2 * rows * units),
        name="mlp",
    )(first, second, *weights)


def add_kernel(kept, arrived, out):
    out[...] = (kept[...] + arrived[...].astype(f32)).astype(bf16)


def add_call(kept, arrived):
    return pl.pallas_call(
        add_kernel,
        out_shape=jax.ShapeDtypeStruct(kept.shape, bf16),
        in_specs=[vmem()] * 2,
        out_specs=vmem(),
        compiler_params=params(8),
        cost_estimate=cost(kept.size, kept.size * 8),
        name="add_partials",
    )(kept, arrived)


def final_kernel(hidden, rate_hbm, kept, *rest):
    arrived, (out, rate, sems) = rest[:-3], rest[-3:]
    copies = fetch([rate_hbm], [rate], sems)
    total = kept[...]
    for part in arrived:
        total = total + part[...].astype(f32)
    state = hidden[...]
    wait(copies)
    state = unit(state + over_rows(rate, state.shape[0]) * (unit(total) - state))
    out[...] = (math.sqrt(D) * state).astype(bf16)


def final_call(hidden, rate, kept, arrived):
    return pl.pallas_call(
        final_kernel,
        out_shape=jax.ShapeDtypeStruct(hidden.shape, bf16),
        in_specs=[vmem(), hbm()] + [vmem()] * (1 + len(arrived)),
        out_specs=pl.BlockSpec(hidden.shape, lambda: (0, 0)),
        scratch_shapes=fetched(rate),
        compiler_params=params(8),
        cost_estimate=cost(hidden.size * 10, hidden.size * 12),
        name="finish",
    )(hidden, rate, kept, *arrived)


def swap(shard, axis, mask):
    length = lax.axis_size(axis)
    return lax.ppermute(shard, axis, [(j, j ^ mask) for j in range(length)])


def body(
    tokens,
    seg_lengths,
    prefix_keys,
    prefix_values,
    w_qkv,
    w_out,
    qk_scale,
    attn_rate,
    w_up,
    w_gate,
    w_down,
    up_scale,
    gate_scale,
    mlp_rate,
):
    extent = lax.axis_size("tok")
    squares = extent // SQ
    place = lax.axis_index("tok").astype(jnp.int32).reshape(1)
    own = tokens[0]
    rows = own.shape[0]

    cached = prefix_call(place, qk_scale, prefix_keys[0], prefix_values[0])
    prefix = [cached[0]] + [swap(cached[m], "tok", m) for m in range(1, SQ)]
    queries, *sent = qkv_call(squares, place, own, qk_scale, w_qkv)
    suffix = [sent[0]] + [swap(sent[m], "tok", m) for m in range(1, SQ)]
    queries = lax.all_to_all(queries.reshape(extent, QD, rows), "tok", 0, 0)
    accum, stats = cached_call(queries, arrive_call(prefix), prefix)
    *parts, w_out = suffix_call(place, seg_lengths, queries, accum, stats, suffix, w_out)
    parts = parts[:1] + [swap(parts[m], "tok", m) for m in range(1, extent)]
    hidden, flat = project_call(place, own, attn_rate, w_out, parts)

    weights = (w_up, w_gate, w_down, up_scale, gate_scale)
    chips = lax.axis_size("grp") // 2
    remote = [swap(flat, "grp", 2 * c) for c in range(1, chips)]
    keep, send = mlp_call(flat, swap(flat, "grp", 1), weights)
    arrived = [swap(send, "grp", 1)]
    for c in range(1, chips):
        data, keep = lax.optimization_barrier((remote[c - 1], keep))
        kept, send = mlp_call(data, swap(data, "grp", 1), weights)
        arrived.append(swap(add_call(kept, swap(send, "grp", 1)), "grp", 2 * c))
    return final_call(hidden, mlp_rate, keep, arrived)[None]


def solution(mesh):
    in_specs = (
        P("grp", "tok", None),
        P("grp", None),
        P("grp", "tok", None),
        P("grp", "tok", None),
        P(),
        P(),
        P(),
        P(),
        P(None, "grp"),
        P(None, "grp"),
        P("grp", None),
        P("grp"),
        P("grp"),
        P(),
    )
    out_specs = P("grp", "tok", None)
    return jax.shard_map(body, mesh=mesh, in_specs=in_specs, out_specs=out_specs, check_vma=False)
```

```python
import functools
import math

import jax
import jax.numpy as jnp
from jax import lax
from jax.experimental import pallas as pl
from jax.experimental.pallas import tpu as pltpu
from jax.sharding import PartitionSpec as P

D = 1280
HEADS = 20
HEAD = 64
EPS = 1e-06
SQ = 4
HQ = HEADS // SQ
QD = HQ * HEAD
LSE = 16
NEG = -1e30
PREFIX_LIMIT = 61
QKV_LIMIT = 50
MIB = 1 << 20

f32 = jnp.float32
bf16 = jnp.bfloat16


def unit(vector):
    return vector * lax.rsqrt(jnp.sum(vector * vector, axis=-1, keepdims=True) + EPS)


def head_unit_t(block, scale):
    dims, rows = block.shape
    per_head = block.reshape(dims // HEAD, HEAD, rows)
    total = jnp.sum(per_head * per_head, axis=1, keepdims=True)
    return (per_head * lax.rsqrt(total + EPS)).reshape(dims, rows) * scale


def params(limit):
    return pltpu.CompilerParams(vmem_limit_bytes=limit * MIB)


def vmem():
    return pl.BlockSpec(memory_space=pltpu.VMEM)


def hbm():
    return pl.BlockSpec(memory_space=pltpu.HBM)


def fetch(sources, targets, sems):
    copies = [
        pltpu.make_async_copy(a, b, sems.at[n]) for n, (a, b) in enumerate(zip(sources, targets))
    ]
    for copy in copies:
        copy.start()
    return copies


def wait(copies):
    for copy in copies:
        copy.wait()


def fetched(*arrays):
    return [pltpu.VMEM(a.shape, a.dtype) for a in arrays] + [
        pltpu.SemaphoreType.DMA((len(arrays),))
    ]


def over_rows(vector, rows):
    tiles = [
        jnp.broadcast_to(vector[c * 128 : (c + 1) * 128], (rows, 128))
        for c in range(vector.shape[0] // 128)
    ]
    return jnp.concatenate(tiles, axis=1)


def smem():
    return pl.BlockSpec(memory_space=pltpu.SMEM)


def cost(flops, nbytes, trans=0):
    return pl.CostEstimate(flops=int(flops), bytes_accessed=int(nbytes), transcendentals=int(trans))


def column(scale, c):
    return jnp.broadcast_to(scale[c * 128 : (c + 1) * 128], (128, 128)).T


def prefix_kernel(place, *rest):
    sources, outs, (parts, scale, keys, values, sems) = rest[:3], rest[3 : 3 + SQ], rest[3 + SQ :]
    copies = fetch(sources, (scale, keys, values), sems)
    rows = keys.shape[0]
    wait(copies[:2])
    for c in range(D // 128):
        cols = slice(c * 128, (c + 1) * 128)
        scale_t = jnp.concatenate([column(scale, c)] * (rows // 128), axis=1)
        split(parts, 0, c, head_unit_t(keys[:, cols].T.astype(f32), scale_t).astype(bf16))
    wait(copies[2:])
    for c in range(D // 128):
        split(parts, QD, c, values[:, c * 128 : (c + 1) * 128].T)
    i = lax.rem(place[0], SQ)
    for m in range(SQ):
        outs[m][...] = parts[jnp.bitwise_xor(i, m)]


def split(out, base, c, block):
    for part in range(0, 128, HEAD):
        row = c * 128 + part
        at = base + row % QD
        out[row // QD, at : at + HEAD, :] = block[part : part + HEAD, :]


def prefix_call(place, scale, keys, values):
    rows = keys.shape[0]
    return pl.pallas_call(
        prefix_kernel,
        out_shape=[jax.ShapeDtypeStruct((2 * QD, rows), bf16)] * SQ,
        in_specs=[smem()] + [hbm()] * 3,
        out_specs=[vmem()] * SQ,
        scratch_shapes=[pltpu.VMEM((SQ, 2 * QD, rows), bf16)] + fetched(scale, keys, values),
        compiler_params=params(PREFIX_LIMIT),
        cost_estimate=cost(5e10, 4 * rows * D * 2),
        name="prefix_prep",
    )(place, scale, keys, values)


def qkv_kernel(squares, place, tokens_hbm, scale_hbm, w_hbm, queries, *rest):
    outs, (parts, tokens, scale, sems, weights, w_sems) = rest[:SQ], rest[SQ:]
    small = fetch((tokens_hbm, scale_hbm), (tokens, scale), sems)
    spans = [pl.ds(p * D, D) for p in range(3)]
    copies = fetch([w_hbm.at[:, p] for p in spans], [weights.at[:, p] for p in spans], w_sems)
    wait(small)
    rows = tokens.shape[0]
    hidden = unit(tokens[...].astype(f32)).astype(bf16)
    columns = [column(scale, c)[:, :rows] for c in range(D // 128)]
    for part in range(3):
        copies[part].wait()
        out = jnp.dot(hidden, weights[:, part * D : (part + 1) * D], preferred_element_type=f32)
        for c in range(D // 128):
            block = out[:, c * 128 : (c + 1) * 128].T
            if part < 2:
                block = head_unit_t(block, columns[c])
            if part == 0:
                block = (block * math.sqrt(HEAD)).astype(bf16)
                for s in range(squares):
                    queries[s * D + c * 128 : s * D + (c + 1) * 128, :] = block
            else:
                split(parts, (part - 1) * QD, c, block.astype(bf16))
    i = lax.rem(place[0], SQ)
    for m in range(SQ):
        outs[m][...] = parts[jnp.bitwise_xor(i, m)]


def qkv_call(squares, place, tokens, scale, weights):
    rows = tokens.shape[0]
    pair = jax.ShapeDtypeStruct((2 * QD, rows), bf16)
    return pl.pallas_call(
        functools.partial(qkv_kernel, squares),
        out_shape=[jax.ShapeDtypeStruct((squares * D, rows), bf16)] + [pair] * SQ,
        in_specs=[smem()] + [hbm()] * 3,
        out_specs=[vmem()] * (1 + SQ),
        scratch_shapes=[
            pltpu.VMEM((SQ, 2 * QD, rows), bf16),
            *fetched(tokens, scale),
            pltpu.VMEM((D, 3 * D), bf16),
            pltpu.SemaphoreType.DMA((3,)),
        ],
        compiler_params=params(QKV_LIMIT),
        cost_estimate=cost(5e10, 3 * D * D * 2),
        name="qkv",
    )(place, tokens, scale, weights)


def arrive_kernel(*refs):
    parts, out = refs[:-1], refs[-1]
    out[...] = functools.reduce(jnp.add, [p[:16, :128].astype(f32) for p in parts])


ARRIVE_COST = 20e9


def arrive_call(parts):
    return pl.pallas_call(
        arrive_kernel,
        out_shape=jax.ShapeDtypeStruct((16, 128), f32),
        in_specs=[vmem()] * len(parts),
        out_specs=vmem(),
        compiler_params=params(2),
        cost_estimate=cost(ARRIVE_COST, 0),
        name="arrive",
    )(*parts)


def cached_kernel(query_all, _, *rest):
    prefix, (accum, stats, keys, values) = rest[:SQ], rest[SQ:]
    extent, _, rows = query_all.shape
    span = prefix[0].shape[1]
    for n, part in enumerate(prefix):
        at = slice(n * span, (n + 1) * span)
        for h in range(HQ):
            keys[h, at, :] = part[h * HEAD : (h + 1) * HEAD, :].T
        values[:, at] = part[QD:, :]
    steps = [(s, h) for s in range(extent // SQ) for h in range(HQ)]
    cuts = [slice(k, k + 2 * span) for k in range(0, SQ * span, 2 * span)]

    def queries(s, h):
        head = slice(h * HEAD, (h + 1) * HEAD)
        return jnp.concatenate([query_all[s * SQ + j, head, :] for j in range(SQ)], axis=1)

    def part_scores(h, cut, query):
        return jnp.dot(keys[h, cut, :], query, preferred_element_type=f32)

    query = queries(0, 0)
    scores = [part_scores(0, cut, query) for cut in cuts]
    for n, (s, h) in enumerate(steps):
        head = slice(h * HEAD, (h + 1) * HEAD)
        top = functools.reduce(jnp.maximum, [jnp.max(x, axis=0, keepdims=True) for x in scores])
        following = steps[n + 1] if n + 1 < len(steps) else None
        if following:
            query = queries(*following)
        ahead, total, blended = [], 0.0, 0.0
        for cut, score in zip(cuts, scores):
            if following:
                ahead.append(part_scores(following[1], cut, query))
            weights = jnp.exp(score - top)
            total = total + jnp.sum(weights, axis=0, keepdims=True)
            blended = blended + jnp.dot(
                values[head, cut], weights.astype(bf16), preferred_element_type=f32
            )
        accum[s, head, :] = blended
        stats[s, h : h + 1, :] = top
        stats[s, 8 + h : 9 + h, :] = total
        scores = ahead


def cached_call(queries, arrived, prefix):
    extent, _, rows = queries.shape
    span = prefix[0].shape[1]
    return pl.pallas_call(
        cached_kernel,
        out_shape=[
            jax.ShapeDtypeStruct((extent // SQ, QD, SQ * rows), f32),
            jax.ShapeDtypeStruct((extent // SQ, 16, SQ * rows), f32),
        ],
        in_specs=[vmem()] * (2 + SQ),
        out_specs=[vmem()] * 2,
        scratch_shapes=[
            pltpu.VMEM((HQ, SQ * span, HEAD), bf16),
            pltpu.VMEM((QD, SQ * span), bf16),
        ],
        compiler_params=params(16),
        cost_estimate=cost(CACHED_COST, 0, 0),
        name="attend_cached",
    )(queries, arrived, *prefix)


CACHED_COST = 1e9


def widen(part, lanes, width, fill):
    rows = part.shape[0]
    pieces = []
    if lanes.start:
        pieces.append(jnp.full((rows, lanes.start), fill, f32))
    pieces.append(part)
    if lanes.stop < width:
        pieces.append(jnp.full((rows, width - lanes.stop), fill, f32))
    return jnp.concatenate(pieces, axis=1)


def suffix_kernel(count, place, lengths, query_all, accum, stats, *rest):
    suffix, w_hbm, rest = rest[:SQ], rest[SQ], rest[SQ + 1 :]
    outs, (w_out, pairs, mixes, sems) = rest[:count], rest[count:]
    copies = fetch([w_hbm], [w_out], sems)
    extent, _, rows = query_all.shape
    i = lax.rem(place[0], SQ)
    square = lax.div(place[0], SQ)
    width = SQ * rows
    for m in range(SQ):
        pairs[jnp.bitwise_xor(i, m)] = suffix[m][...]
    for shift in range(extent // SQ):
        query_square = jnp.bitwise_xor(square, shift)
        position = query_square * width + lax.broadcasted_iota(jnp.int32, (1, width), 1)
        first = jnp.zeros((1, width), jnp.int32)
        bound = jnp.int32(0)
        for r in range(lengths.shape[1]):
            bound = bound + lengths[0, r]
            first = jnp.where(position >= bound, bound, first)
        windows = [(SQ - 2, 0, 1), (SQ - 1, 0, 2)]
        if not shift:
            windows = [(j, j, min(SQ, j + 3)) for j in range(SQ)]
        masks = []
        for block, begin, end in windows:
            lanes = slice(begin * rows, end * rows)
            key_at = (square * SQ + block) * rows + lax.broadcasted_iota(
                jnp.int32, (rows, lanes.stop - lanes.start), 0
            )
            masks.append((key_at >= first[:, lanes]) & (key_at <= position[:, lanes]))
        scores = []
        for h in range(HQ):
            head = slice(h * HEAD, (h + 1) * HEAD)
            query = [query_all[query_square * SQ + j, head, :] for j in range(windows[-1][2])]
            for (block, begin, end), mask in zip(windows, masks):
                score = jnp.dot(
                    pairs[block, head, :].T,
                    jnp.concatenate(query[begin:end], axis=1),
                    preferred_element_type=f32,
                )
                scores.append(jnp.where(mask, score, NEG))
        states = []
        for h in range(HQ):
            cached_top = stats[query_square, h : h + 1, :]
            top = cached_top
            part = scores[h * len(windows) : (h + 1) * len(windows)]
            for score, (block, begin, end) in zip(part, windows):
                lanes = slice(begin * rows, end * rows)
                level = jnp.max(score, axis=0, keepdims=True)
                top = jnp.maximum(top, widen(level, lanes, width, NEG))
            shrink = jnp.exp(cached_top - top)
            total = stats[query_square, 8 + h : 9 + h, :] * shrink
            weights = []
            for score, (block, begin, end) in zip(part, windows):
                lanes = slice(begin * rows, end * rows)
                weight = jnp.exp(score - top[:, lanes])
                total = total + widen(jnp.sum(weight, axis=0, keepdims=True), lanes, width, 0.0)
                weights.append(weight.astype(bf16))
            states.append((top, shrink, total, weights))
        for h, (top, shrink, total, weights) in enumerate(states):
            head = slice(h * HEAD, (h + 1) * HEAD)
            head_v = slice(QD + h * HEAD, QD + (h + 1) * HEAD)
            mixed = accum[query_square, head, :] * shrink
            for weight, (block, begin, end) in zip(weights, windows):
                lanes = slice(begin * rows, end * rows)
                blended = jnp.dot(pairs[block, head_v, :], weight, preferred_element_type=f32)
                mixed = mixed + widen(blended, lanes, width, 0.0)
            mixes[head, :] = mixed * (1.0 / total)
            level = top + jnp.log(total)
            high = level.astype(bf16).astype(f32)
            middle = (level - high).astype(bf16).astype(f32)
            for n, piece in enumerate((high, middle, level - high - middle)):
                row = QD + n * HQ + h
                mixes[row : row + 1, :] = piece
        mixes[QD + LSE - 1 :, :] = jnp.zeros((1, width), f32)
        for m in range(SQ):
            lanes = pl.ds(pl.multiple_of(jnp.bitwise_xor(i, m) * rows, rows), rows)
            outs[shift * SQ + m][...] = mixes[:, lanes].astype(bf16)
    wait(copies)


def suffix_call(place, lengths, queries, accum, stats, suffix, w_out):
    extent, _, rows = queries.shape
    return pl.pallas_call(
        functools.partial(suffix_kernel, extent),
        out_shape=[jax.ShapeDtypeStruct((QD + LSE, rows), bf16)] * extent
        + [jax.ShapeDtypeStruct(w_out.shape, bf16)],
        in_specs=[smem(), smem()] + [vmem()] * (3 + SQ) + [hbm()],
        out_specs=[vmem()] * (extent + 1),
        scratch_shapes=[
            pltpu.VMEM((SQ, 2 * QD, rows), bf16),
            pltpu.VMEM((QD + LSE, SQ * rows), f32),
            pltpu.SemaphoreType.DMA((1,)),
        ],
        compiler_params=params(8),
        cost_estimate=cost(2e10, 8 * MIB, 0),
        name="attend_suffix",
    )(place, lengths, queries, accum, stats, *suffix, w_out)


def project_kernel(order, place, tokens_hbm, rate_hbm, w_out, *rest):
    count = len(order)
    arrived, rest = rest[:count], rest[count:]
    hidden_out, flat_out, mix, parts, tokens, rate, sems = rest
    copies = fetch((tokens_hbm, rate_hbm), (tokens, rate), sems)
    squares = count // SQ
    i = lax.rem(place[0], SQ)
    for m, part in zip(order, arrived):
        parts[m // SQ * SQ + jnp.bitwise_xor(i, m % SQ)] = part[...]
    for j in range(SQ):
        group = [parts.at[s * SQ + j] for s in range(squares)]
        levels = []
        for part in group:
            pieces = part[QD:, :].astype(f32)
            levels.append(pieces[:HQ] + pieces[HQ : 2 * HQ] + pieces[2 * HQ : 3 * HQ])
        top = functools.reduce(jnp.maximum, levels)
        weights = [jnp.exp(v - top) for v in levels]
        inverse = 1.0 / functools.reduce(jnp.add, weights)
        weights = [w * inverse for w in weights]
        for h in range(HQ):
            head = slice(h * HEAD, (h + 1) * HEAD)
            mixed = functools.reduce(
                jnp.add, [w[h : h + 1, :] * p[head, :].astype(f32) for w, p in zip(weights, group)]
            )
            at = j * QD + h * HEAD
            mix[at : at + HEAD, :] = mixed.astype(bf16)
    wait(copies)
    hidden = unit(tokens[...].astype(f32))
    attn = jnp.concatenate(
        [mix[c * 128 : (c + 1) * 128, :].astype(f32).T.astype(bf16) for c in range(D // 128)], axis=1
    )
    attended = unit(jnp.dot(attn, w_out[...], preferred_element_type=f32))
    hidden = unit(hidden + over_rows(rate, hidden.shape[0]) * (attended - hidden))
    hidden_out[...] = hidden
    flat_out[...] = hidden.astype(bf16)


def project_call(place, tokens, rate, w_out, parts):
    rows = tokens.shape[0]
    return pl.pallas_call(
        functools.partial(project_kernel, list(parts)),
        out_shape=[jax.ShapeDtypeStruct((rows, D), f32), jax.ShapeDtypeStruct((rows, D), bf16)],
        in_specs=[smem(), hbm(), hbm()] + [vmem()] * (1 + len(parts)),
        out_specs=[vmem()] * 2,
        scratch_shapes=[
            pltpu.VMEM((D, rows), bf16),
            pltpu.VMEM((len(parts), *parts[0].shape), bf16),
            *fetched(tokens, rate),
        ],
        compiler_params=params(8),
        cost_estimate=cost(2 * rows * D * D, D * D * 2),
        name="project",
    )(place, tokens, rate, w_out, *parts.values())


def mlp_kernel(first, second, w_up, w_gate, w_down, up_scale, gate_scale, keep, send):
    rows = first.shape[0]
    data = jnp.concatenate([first[...], second[...]], axis=0)
    up = jnp.dot(data, w_up[...], preferred_element_type=f32) * over_rows(up_scale, 2 * rows)
    gate = jnp.dot(data, w_gate[...], preferred_element_type=f32)
    gate = gate * (over_rows(gate_scale, 2 * rows) * math.sqrt(D))
    act = (up * (gate / (1.0 + jnp.exp(-gate)))).astype(bf16)
    part = jnp.dot(act, w_down[...], preferred_element_type=f32)
    keep[...] = part[:rows, :]
    send[...] = part[rows:, :].astype(bf16)


def mlp_call(first, second, weights):
    rows = first.shape[0]
    units = weights[0].shape[1]
    return pl.pallas_call(
        mlp_kernel,
        out_shape=[jax.ShapeDtypeStruct((rows, D), f32), jax.ShapeDtypeStruct((rows, D), bf16)],
        in_specs=[vmem()] * 7,
        out_specs=[vmem()] * 2,
        compiler_params=params(12),
        cost_estimate=cost(2 * 2 * rows * D * units * 3, 3 * D * units * 2, 2 * rows * units),
        name="mlp",
    )(first, second, *weights)


def add_kernel(kept, arrived, out):
    out[...] = (kept[...] + arrived[...].astype(f32)).astype(bf16)


def add_call(kept, arrived):
    return pl.pallas_call(
        add_kernel,
        out_shape=jax.ShapeDtypeStruct(kept.shape, bf16),
        in_specs=[vmem()] * 2,
        out_specs=vmem(),
        compiler_params=params(8),
        cost_estimate=cost(kept.size, kept.size * 8),
        name="add_partials",
    )(kept, arrived)


def final_kernel(hidden, rate_hbm, kept, *rest):
    arrived, (out, rate, sems) = rest[:-3], rest[-3:]
    copies = fetch([rate_hbm], [rate], sems)
    total = kept[...]
    for part in arrived:
        total = total + part[...].astype(f32)
    state = hidden[...]
    wait(copies)
    state = unit(state + over_rows(rate, state.shape[0]) * (unit(total) - state))
    out[...] = (math.sqrt(D) * state).astype(bf16)


def final_call(hidden, rate, kept, arrived):
    return pl.pallas_call(
        final_kernel,
        out_shape=jax.ShapeDtypeStruct(hidden.shape, bf16),
        in_specs=[vmem(), hbm()] + [vmem()] * (1 + len(arrived)),
        out_specs=pl.BlockSpec(hidden.shape, lambda: (0, 0)),
        scratch_shapes=fetched(rate),
        compiler_params=params(8),
        cost_estimate=cost(hidden.size * 10, hidden.size * 12),
        name="finish",
    )(hidden, rate, kept, *arrived)


def swap(shard, axis, mask):
    length = lax.axis_size(axis)
    return lax.ppermute(shard, axis, [(j, j ^ mask) for j in range(length)])


def body(
    tokens,
    seg_lengths,
    prefix_keys,
    prefix_values,
    w_qkv,
    w_out,
    qk_scale,
    attn_rate,
    w_up,
    w_gate,
    w_down,
    up_scale,
    gate_scale,
    mlp_rate,
):
    extent = lax.axis_size("tok")
    squares = extent // SQ
    place = lax.axis_index("tok").astype(jnp.int32).reshape(1)
    own = tokens[0]
    rows = own.shape[0]

    cached = prefix_call(place, qk_scale, prefix_keys[0], prefix_values[0])
    prefix = [cached[0]] + [swap(cached[m], "tok", m) for m in range(1, SQ)]
    queries, *sent = qkv_call(squares, place, own, qk_scale, w_qkv)
    suffix = [sent[0]] + [swap(sent[m], "tok", m) for m in range(1, SQ)]
    queries = lax.all_to_all(queries.reshape(extent, QD, rows), "tok", 0, 0)
    accum, stats = cached_call(queries, arrive_call(prefix), prefix)
    *parts, w_out = suffix_call(place, seg_lengths, queries, accum, stats, suffix, w_out)
    order = [1, *range(SQ, extent), *range(SQ - 1, 1, -1)]
    parts = {m: swap(parts[m], "tok", m) for m in order} | {0: parts[0]}
    hidden, flat = project_call(place, own, attn_rate, w_out, parts)

    weights = (w_up, w_gate, w_down, up_scale, gate_scale)
    chips = lax.axis_size("grp") // 2
    remote = [swap(flat, "grp", 2 * c) for c in range(1, chips)]
    keep, send = mlp_call(flat, swap(flat, "grp", 1), weights)
    arrived = [swap(send, "grp", 1)]
    for c in range(1, chips):
        data, keep = lax.optimization_barrier((remote[c - 1], keep))
        kept, send = mlp_call(data, swap(data, "grp", 1), weights)
        arrived.append(swap(add_call(kept, swap(send, "grp", 1)), "grp", 2 * c))
    return final_call(hidden, mlp_rate, keep, arrived)[None]


def solution(mesh):
    in_specs = (
        P("grp", "tok", None),
        P("grp", None),
        P("grp", "tok", None),
        P("grp", "tok", None),
        P(),
        P(),
        P(),
        P(),
        P(None, "grp"),
        P(None, "grp"),
        P("grp", None),
        P("grp"),
        P("grp"),
        P(),
    )
    out_specs = P("grp", "tok", None)
    return jax.shard_map(body, mesh=mesh, in_specs=in_specs, out_specs=out_specs, check_vma=False)
```

```python
import functools
import math

import jax
import jax.numpy as jnp
from jax import lax
from jax.experimental import pallas as pl
from jax.experimental.pallas import tpu as pltpu
from jax.sharding import PartitionSpec as P

D = 1280
HEADS = 20
HEAD = 64
EPS = 1e-06
SQ = 4
HQ = HEADS // SQ
QD = HQ * HEAD
LSE = 16
NEG = -1e30
PREFIX_LIMIT = 61
QKV_LIMIT = 50
MIB = 1 << 20

f32 = jnp.float32
bf16 = jnp.bfloat16


def unit(vector):
    return vector * lax.rsqrt(jnp.sum(vector * vector, axis=-1, keepdims=True) + EPS)


def head_unit_t(block, scale):
    dims, rows = block.shape
    per_head = block.reshape(dims // HEAD, HEAD, rows)
    total = jnp.sum(per_head * per_head, axis=1, keepdims=True)
    return (per_head * lax.rsqrt(total + EPS)).reshape(dims, rows) * scale


def params(limit):
    return pltpu.CompilerParams(vmem_limit_bytes=limit * MIB)


def vmem():
    return pl.BlockSpec(memory_space=pltpu.VMEM)


def hbm():
    return pl.BlockSpec(memory_space=pltpu.HBM)


def fetch(sources, targets, sems):
    copies = [
        pltpu.make_async_copy(a, b, sems.at[n]) for n, (a, b) in enumerate(zip(sources, targets))
    ]
    for copy in copies:
        copy.start()
    return copies


def wait(copies):
    for copy in copies:
        copy.wait()


def fetched(*arrays):
    return [pltpu.VMEM(a.shape, a.dtype) for a in arrays] + [
        pltpu.SemaphoreType.DMA((len(arrays),))
    ]


def over_rows(vector, rows):
    tiles = [
        jnp.broadcast_to(vector[c * 128 : (c + 1) * 128], (rows, 128))
        for c in range(vector.shape[0] // 128)
    ]
    return jnp.concatenate(tiles, axis=1)


def smem():
    return pl.BlockSpec(memory_space=pltpu.SMEM)


def cost(flops, nbytes, trans=0):
    return pl.CostEstimate(flops=int(flops), bytes_accessed=int(nbytes), transcendentals=int(trans))


def column(scale, c):
    return jnp.broadcast_to(scale[c * 128 : (c + 1) * 128], (128, 128)).T


def prefix_kernel(place, *rest):
    sources, outs, rest = rest[:3], rest[3 : 3 + SQ], rest[3 + SQ :]
    *parts, scale, keys, values, sems, out_sems = rest
    i = lax.rem(place[0], SQ)

    def leave(half):
        return fetch(
            [parts[half].at[jnp.bitwise_xor(i, m)] for m in range(SQ)],
            [out.at[pl.ds(half * QD, QD), :] for out in outs],
            out_sems.at[half],
        )

    copies = fetch(sources, (scale, keys, values), sems)
    rows = keys.shape[0]
    wait(copies[:2])
    for c in range(D // 128):
        cols = slice(c * 128, (c + 1) * 128)
        scale_t = jnp.concatenate([column(scale, c)] * (rows // 128), axis=1)
        split(parts[0], 0, c, head_unit_t(keys[:, cols].T.astype(f32), scale_t).astype(bf16))
    left = leave(0)
    wait(copies[2:])
    for c in range(D // 128):
        split(parts[1], 0, c, values[:, c * 128 : (c + 1) * 128].T)
    wait(left + leave(1))


def split(out, base, c, block):
    for part in range(0, 128, HEAD):
        row = c * 128 + part
        at = base + row % QD
        out[row // QD, at : at + HEAD, :] = block[part : part + HEAD, :]


def prefix_call(place, scale, keys, values):
    rows = keys.shape[0]
    return pl.pallas_call(
        prefix_kernel,
        out_shape=[jax.ShapeDtypeStruct((2 * QD, rows), bf16)] * SQ,
        in_specs=[smem()] + [hbm()] * 3,
        out_specs=[hbm()] * SQ,
        scratch_shapes=[pltpu.VMEM((SQ, QD, rows), bf16)] * 2
        + fetched(scale, keys, values)
        + [pltpu.SemaphoreType.DMA((2, SQ))],
        compiler_params=params(PREFIX_LIMIT),
        cost_estimate=cost(5e10, 4 * rows * D * 2),
        name="prefix_prep",
    )(place, scale, keys, values)


def qkv_kernel(squares, place, tokens_hbm, scale_hbm, w_hbm, queries, *rest):
    outs, (parts, tokens, scale, sems, weights, w_sems) = rest[:SQ], rest[SQ:]
    small = fetch((tokens_hbm, scale_hbm), (tokens, scale), sems)
    spans = [pl.ds(p * D, D) for p in range(3)]
    copies = fetch([w_hbm.at[:, p] for p in spans], [weights.at[:, p] for p in spans], w_sems)
    wait(small)
    rows = tokens.shape[0]
    hidden = unit(tokens[...].astype(f32)).astype(bf16)
    columns = [column(scale, c)[:, :rows] for c in range(D // 128)]
    for part in range(3):
        copies[part].wait()
        out = jnp.dot(hidden, weights[:, part * D : (part + 1) * D], preferred_element_type=f32)
        for c in range(D // 128):
            block = out[:, c * 128 : (c + 1) * 128].T
            if part < 2:
                block = head_unit_t(block, columns[c])
            if part == 0:
                block = (block * math.sqrt(HEAD)).astype(bf16)
                for s in range(squares):
                    queries[s * D + c * 128 : s * D + (c + 1) * 128, :] = block
            else:
                split(parts, (part - 1) * QD, c, block.astype(bf16))
    i = lax.rem(place[0], SQ)
    for m in range(SQ):
        outs[m][...] = parts[jnp.bitwise_xor(i, m)]


def qkv_call(squares, place, tokens, scale, weights):
    rows = tokens.shape[0]
    pair = jax.ShapeDtypeStruct((2 * QD, rows), bf16)
    return pl.pallas_call(
        functools.partial(qkv_kernel, squares),
        out_shape=[jax.ShapeDtypeStruct((squares * D, rows), bf16)] + [pair] * SQ,
        in_specs=[smem()] + [hbm()] * 3,
        out_specs=[vmem()] * (1 + SQ),
        scratch_shapes=[
            pltpu.VMEM((SQ, 2 * QD, rows), bf16),
            *fetched(tokens, scale),
            pltpu.VMEM((D, 3 * D), bf16),
            pltpu.SemaphoreType.DMA((3,)),
        ],
        compiler_params=params(QKV_LIMIT),
        cost_estimate=cost(5e10, 3 * D * D * 2),
        name="qkv",
    )(place, tokens, scale, weights)


def arrive_kernel(*refs):
    parts, out = refs[:-1], refs[-1]
    out[...] = functools.reduce(jnp.add, [p[:16, :128].astype(f32) for p in parts])


ARRIVE_COST = 20e9


def arrive_call(parts):
    return pl.pallas_call(
        arrive_kernel,
        out_shape=jax.ShapeDtypeStruct((16, 128), f32),
        in_specs=[vmem()] * len(parts),
        out_specs=vmem(),
        compiler_params=params(2),
        cost_estimate=cost(ARRIVE_COST, 0),
        name="arrive",
    )(*parts)


def cached_kernel(query_all, _, *rest):
    prefix, (accum, stats, keys, values) = rest[:SQ], rest[SQ:]
    extent, _, rows = query_all.shape
    span = prefix[0].shape[1]
    for n, part in enumerate(prefix):
        at = slice(n * span, (n + 1) * span)
        for h in range(HQ):
            keys[h, at, :] = part[h * HEAD : (h + 1) * HEAD, :].T
        values[:, at] = part[QD:, :]
    steps = [(s, h) for s in range(extent // SQ) for h in range(HQ)]
    cuts = [slice(k, k + 2 * span) for k in range(0, SQ * span, 2 * span)]

    def queries(s, h):
        head = slice(h * HEAD, (h + 1) * HEAD)
        return jnp.concatenate([query_all[s * SQ + j, head, :] for j in range(SQ)], axis=1)

    def part_scores(h, cut, query):
        return jnp.dot(keys[h, cut, :], query, preferred_element_type=f32)

    query = queries(0, 0)
    scores = [part_scores(0, cut, query) for cut in cuts]
    for n, (s, h) in enumerate(steps):
        head = slice(h * HEAD, (h + 1) * HEAD)
        top = functools.reduce(jnp.maximum, [jnp.max(x, axis=0, keepdims=True) for x in scores])
        following = steps[n + 1] if n + 1 < len(steps) else None
        if following:
            query = queries(*following)
        ahead, total, blended = [], 0.0, 0.0
        for cut, score in zip(cuts, scores):
            if following:
                ahead.append(part_scores(following[1], cut, query))
            weights = jnp.exp(score - top)
            total = total + jnp.sum(weights, axis=0, keepdims=True)
            blended = blended + jnp.dot(
                values[head, cut], weights.astype(bf16), preferred_element_type=f32
            )
        accum[s, head, :] = blended
        stats[s, h : h + 1, :] = top
        stats[s, 8 + h : 9 + h, :] = total
        scores = ahead


def cached_call(queries, arrived, prefix):
    extent, _, rows = queries.shape
    span = prefix[0].shape[1]
    return pl.pallas_call(
        cached_kernel,
        out_shape=[
            jax.ShapeDtypeStruct((extent // SQ, QD, SQ * rows), f32),
            jax.ShapeDtypeStruct((extent // SQ, 16, SQ * rows), f32),
        ],
        in_specs=[vmem()] * (2 + SQ),
        out_specs=[vmem()] * 2,
        scratch_shapes=[
            pltpu.VMEM((HQ, SQ * span, HEAD), bf16),
            pltpu.VMEM((QD, SQ * span), bf16),
        ],
        compiler_params=params(16),
        cost_estimate=cost(CACHED_COST, 0, 0),
        name="attend_cached",
    )(queries, arrived, *prefix)


CACHED_COST = 1e9


def widen(part, lanes, width, fill):
    rows = part.shape[0]
    pieces = []
    if lanes.start:
        pieces.append(jnp.full((rows, lanes.start), fill, f32))
    pieces.append(part)
    if lanes.stop < width:
        pieces.append(jnp.full((rows, width - lanes.stop), fill, f32))
    return jnp.concatenate(pieces, axis=1)


def suffix_kernel(count, place, lengths, query_all, accum, stats, *rest):
    suffix, w_hbm, rest = rest[:SQ], rest[SQ], rest[SQ + 1 :]
    outs, (w_out, pairs, mixes, sems) = rest[:count], rest[count:]
    copies = fetch([w_hbm], [w_out], sems)
    extent, _, rows = query_all.shape
    i = lax.rem(place[0], SQ)
    square = lax.div(place[0], SQ)
    width = SQ * rows
    for m in range(SQ):
        pairs[jnp.bitwise_xor(i, m)] = suffix[m][...]
    for shift in range(extent // SQ):
        query_square = jnp.bitwise_xor(square, shift)
        position = query_square * width + lax.broadcasted_iota(jnp.int32, (1, width), 1)
        first = jnp.zeros((1, width), jnp.int32)
        bound = jnp.int32(0)
        for r in range(lengths.shape[1]):
            bound = bound + lengths[0, r]
            first = jnp.where(position >= bound, bound, first)
        windows = [(SQ - 2, 0, 1), (SQ - 1, 0, 2)]
        if not shift:
            windows = [(j, j, min(SQ, j + 3)) for j in range(SQ)]
        masks = []
        for block, begin, end in windows:
            lanes = slice(begin * rows, end * rows)
            key_at = (square * SQ + block) * rows + lax.broadcasted_iota(
                jnp.int32, (rows, lanes.stop - lanes.start), 0
            )
            allowed = (key_at >= first[:, lanes]) & (key_at <= position[:, lanes])
            masks.append(jnp.where(allowed, 0.0, NEG))
        scores = []
        for h in range(HQ):
            head = slice(h * HEAD, (h + 1) * HEAD)
            query = [query_all[query_square * SQ + j, head, :] for j in range(windows[-1][2])]
            for (block, begin, end), mask in zip(windows, masks):
                score = jnp.dot(
                    pairs[block, head, :].T,
                    jnp.concatenate(query[begin:end], axis=1),
                    preferred_element_type=f32,
                )
                scores.append(score + mask)
        states = []
        for h in range(HQ):
            cached_top = stats[query_square, h : h + 1, :]
            top = cached_top
            part = scores[h * len(windows) : (h + 1) * len(windows)]
            for score, (block, begin, end) in zip(part, windows):
                lanes = slice(begin * rows, end * rows)
                level = jnp.max(score, axis=0, keepdims=True)
                top = jnp.maximum(top, widen(level, lanes, width, NEG))
            shrink = jnp.exp(cached_top - top)
            total = stats[query_square, 8 + h : 9 + h, :] * shrink
            weights = []
            for score, (block, begin, end) in zip(part, windows):
                lanes = slice(begin * rows, end * rows)
                weight = jnp.exp(score - top[:, lanes])
                total = total + widen(jnp.sum(weight, axis=0, keepdims=True), lanes, width, 0.0)
                weights.append(weight.astype(bf16))
            states.append((top, shrink, total, weights))
        for h, (top, shrink, total, weights) in enumerate(states):
            head = slice(h * HEAD, (h + 1) * HEAD)
            head_v = slice(QD + h * HEAD, QD + (h + 1) * HEAD)
            mixed = accum[query_square, head, :] * shrink
            for weight, (block, begin, end) in zip(weights, windows):
                lanes = slice(begin * rows, end * rows)
                blended = jnp.dot(pairs[block, head_v, :], weight, preferred_element_type=f32)
                mixed = mixed + widen(blended, lanes, width, 0.0)
            mixes[head, :] = mixed * (1.0 / total)
            level = top + jnp.log(total)
            high = level.astype(bf16).astype(f32)
            middle = (level - high).astype(bf16).astype(f32)
            for n, piece in enumerate((high, middle, level - high - middle)):
                row = QD + n * HQ + h
                mixes[row : row + 1, :] = piece
        mixes[QD + LSE - 1 :, :] = jnp.zeros((1, width), f32)
        for m in range(SQ):
            lanes = pl.ds(pl.multiple_of(jnp.bitwise_xor(i, m) * rows, rows), rows)
            outs[shift * SQ + m][...] = mixes[:, lanes].astype(bf16)
    wait(copies)


def suffix_call(place, lengths, queries, accum, stats, suffix, w_out):
    extent, _, rows = queries.shape
    return pl.pallas_call(
        functools.partial(suffix_kernel, extent),
        out_shape=[jax.ShapeDtypeStruct((QD + LSE, rows), bf16)] * extent
        + [jax.ShapeDtypeStruct(w_out.shape, bf16)],
        in_specs=[smem(), smem()] + [vmem()] * (3 + SQ) + [hbm()],
        out_specs=[vmem()] * (extent + 1),
        scratch_shapes=[
            pltpu.VMEM((SQ, 2 * QD, rows), bf16),
            pltpu.VMEM((QD + LSE, SQ * rows), f32),
            pltpu.SemaphoreType.DMA((1,)),
        ],
        compiler_params=params(8),
        cost_estimate=cost(2e10, 8 * MIB, 0),
        name="attend_suffix",
    )(place, lengths, queries, accum, stats, *suffix, w_out)


def project_kernel(order, place, tokens_hbm, rate_hbm, w_out, *rest):
    count = len(order)
    arrived, rest = rest[:count], rest[count:]
    hidden_out, flat_out, mix, parts, tokens, rate, sems = rest
    copies = fetch((tokens_hbm, rate_hbm), (tokens, rate), sems)
    squares = count // SQ
    i = lax.rem(place[0], SQ)
    for m, part in zip(order, arrived):
        parts[m // SQ * SQ + jnp.bitwise_xor(i, m % SQ)] = part[...]
    for j in range(SQ):
        group = [parts.at[s * SQ + j] for s in range(squares)]
        levels = []
        for part in group:
            pieces = part[QD:, :].astype(f32)
            levels.append(pieces[:HQ] + pieces[HQ : 2 * HQ] + pieces[2 * HQ : 3 * HQ])
        top = functools.reduce(jnp.maximum, levels)
        weights = [jnp.exp(v - top) for v in levels]
        inverse = 1.0 / functools.reduce(jnp.add, weights)
        weights = [w * inverse for w in weights]
        for h in range(HQ):
            head = slice(h * HEAD, (h + 1) * HEAD)
            mixed = functools.reduce(
                jnp.add, [w[h : h + 1, :] * p[head, :].astype(f32) for w, p in zip(weights, group)]
            )
            at = j * QD + h * HEAD
            mix[at : at + HEAD, :] = mixed.astype(bf16)
    wait(copies)
    hidden = unit(tokens[...].astype(f32))
    attn = jnp.concatenate(
        [mix[c * 128 : (c + 1) * 128, :].astype(f32).T.astype(bf16) for c in range(D // 128)], axis=1
    )
    attended = unit(jnp.dot(attn, w_out[...], preferred_element_type=f32))
    hidden = unit(hidden + over_rows(rate, hidden.shape[0]) * (attended - hidden))
    hidden_out[...] = hidden
    flat_out[...] = hidden.astype(bf16)


def project_call(place, tokens, rate, w_out, parts):
    rows = tokens.shape[0]
    return pl.pallas_call(
        functools.partial(project_kernel, list(parts)),
        out_shape=[jax.ShapeDtypeStruct((rows, D), f32), jax.ShapeDtypeStruct((rows, D), bf16)],
        in_specs=[smem(), hbm(), hbm()] + [vmem()] * (1 + len(parts)),
        out_specs=[vmem()] * 2,
        scratch_shapes=[
            pltpu.VMEM((D, rows), bf16),
            pltpu.VMEM((len(parts), *parts[0].shape), bf16),
            *fetched(tokens, rate),
        ],
        compiler_params=params(8),
        cost_estimate=cost(2 * rows * D * D, D * D * 2),
        name="project",
    )(place, tokens, rate, w_out, *parts.values())


def mlp_kernel(first, second, w_up, w_gate, w_down, up_scale, gate_scale, keep, send):
    rows = first.shape[0]
    data = jnp.concatenate([first[...], second[...]], axis=0)
    up = jnp.dot(data, w_up[...], preferred_element_type=f32) * over_rows(up_scale, 2 * rows)
    gate = jnp.dot(data, w_gate[...], preferred_element_type=f32)
    gate = gate * (over_rows(gate_scale, 2 * rows) * math.sqrt(D))
    act = (up * (gate / (1.0 + jnp.exp(-gate)))).astype(bf16)
    part = jnp.dot(act, w_down[...], preferred_element_type=f32)
    keep[...] = part[:rows, :]
    send[...] = part[rows:, :].astype(bf16)


def mlp_call(first, second, weights):
    rows = first.shape[0]
    units = weights[0].shape[1]
    return pl.pallas_call(
        mlp_kernel,
        out_shape=[jax.ShapeDtypeStruct((rows, D), f32), jax.ShapeDtypeStruct((rows, D), bf16)],
        in_specs=[vmem()] * 7,
        out_specs=[vmem()] * 2,
        compiler_params=params(12),
        cost_estimate=cost(2 * 2 * rows * D * units * 3, 3 * D * units * 2, 2 * rows * units),
        name="mlp",
    )(first, second, *weights)


def add_kernel(kept, arrived, out):
    out[...] = (kept[...] + arrived[...].astype(f32)).astype(bf16)


def add_call(kept, arrived):
    return pl.pallas_call(
        add_kernel,
        out_shape=jax.ShapeDtypeStruct(kept.shape, bf16),
        in_specs=[vmem()] * 2,
        out_specs=vmem(),
        compiler_params=params(8),
        cost_estimate=cost(kept.size, kept.size * 8),
        name="add_partials",
    )(kept, arrived)


def final_kernel(hidden, rate_hbm, kept, *rest):
    arrived, (out, rate, sems) = rest[:-3], rest[-3:]
    copies = fetch([rate_hbm], [rate], sems)
    total = kept[...]
    for part in arrived:
        total = total + part[...].astype(f32)
    state = hidden[...]
    wait(copies)
    state = unit(state + over_rows(rate, state.shape[0]) * (unit(total) - state))
    out[...] = (math.sqrt(D) * state).astype(bf16)


def final_call(hidden, rate, kept, arrived):
    return pl.pallas_call(
        final_kernel,
        out_shape=jax.ShapeDtypeStruct(hidden.shape, bf16),
        in_specs=[vmem(), hbm()] + [vmem()] * (1 + len(arrived)),
        out_specs=pl.BlockSpec(hidden.shape, lambda: (0, 0)),
        scratch_shapes=fetched(rate),
        compiler_params=params(8),
        cost_estimate=cost(hidden.size * 10, hidden.size * 12),
        name="finish",
    )(hidden, rate, kept, *arrived)


def swap(shard, axis, mask):
    length = lax.axis_size(axis)
    return lax.ppermute(shard, axis, [(j, j ^ mask) for j in range(length)])


def body(
    tokens,
    seg_lengths,
    prefix_keys,
    prefix_values,
    w_qkv,
    w_out,
    qk_scale,
    attn_rate,
    w_up,
    w_gate,
    w_down,
    up_scale,
    gate_scale,
    mlp_rate,
):
    extent = lax.axis_size("tok")
    squares = extent // SQ
    place = lax.axis_index("tok").astype(jnp.int32).reshape(1)
    own = tokens[0]
    rows = own.shape[0]

    cached = prefix_call(place, qk_scale, prefix_keys[0], prefix_values[0])
    prefix = [cached[0]] + [swap(cached[m], "tok", m) for m in range(1, SQ)]
    queries, *sent = qkv_call(squares, place, own, qk_scale, w_qkv)
    suffix = [sent[0]] + [swap(sent[m], "tok", m) for m in range(1, SQ)]
    queries = lax.all_to_all(queries.reshape(extent, QD, rows), "tok", 0, 0)
    accum, stats = cached_call(queries, arrive_call(prefix), prefix)
    *parts, w_out = suffix_call(place, seg_lengths, queries, accum, stats, suffix, w_out)
    order = [1, *range(SQ, extent), *range(SQ - 1, 1, -1)]
    parts = {m: swap(parts[m], "tok", m) for m in order} | {0: parts[0]}
    hidden, flat = project_call(place, own, attn_rate, w_out, parts)

    weights = (w_up, w_gate, w_down, up_scale, gate_scale)
    chips = lax.axis_size("grp") // 2
    remote = [swap(flat, "grp", 2 * c) for c in range(1, chips)]
    keep, send = mlp_call(flat, swap(flat, "grp", 1), weights)
    arrived = [swap(send, "grp", 1)]
    for c in range(1, chips):
        data, keep = lax.optimization_barrier((remote[c - 1], keep))
        kept, send = mlp_call(data, swap(data, "grp", 1), weights)
        arrived.append(swap(add_call(kept, swap(send, "grp", 1)), "grp", 2 * c))
    return final_call(hidden, mlp_rate, keep, arrived)[None]


def solution(mesh):
    in_specs = (
        P("grp", "tok", None),
        P("grp", None),
        P("grp", "tok", None),
        P("grp", "tok", None),
        P(),
        P(),
        P(),
        P(),
        P(None, "grp"),
        P(None, "grp"),
        P("grp", None),
        P("grp"),
        P("grp"),
        P(),
    )
    out_specs = P("grp", "tok", None)
    return jax.shard_map(body, mesh=mesh, in_specs=in_specs, out_specs=out_specs, check_vma=False)
```

```python
import functools
import math

import jax
import jax.numpy as jnp
from jax import lax
from jax.experimental import pallas as pl
from jax.experimental.pallas import tpu as pltpu
from jax.sharding import PartitionSpec as P

D = 1280
HEADS = 20
HEAD = 64
EPS = 1e-06
SQ = 4
HQ = HEADS // SQ
QD = HQ * HEAD
LSE = 16
NEG = -1e30
PREFIX_LIMIT = 61
QKV_LIMIT = 50
MIB = 1 << 20

f32 = jnp.float32
bf16 = jnp.bfloat16


def unit(vector):
    return vector * lax.rsqrt(jnp.sum(vector * vector, axis=-1, keepdims=True) + EPS)


def head_unit_t(block, scale):
    dims, rows = block.shape
    per_head = block.reshape(dims // HEAD, HEAD, rows)
    total = jnp.sum(per_head * per_head, axis=1, keepdims=True)
    return (per_head * lax.rsqrt(total + EPS)).reshape(dims, rows) * scale


def params(limit):
    return pltpu.CompilerParams(vmem_limit_bytes=limit * MIB)


def vmem():
    return pl.BlockSpec(memory_space=pltpu.VMEM)


def hbm():
    return pl.BlockSpec(memory_space=pltpu.HBM)


def fetch(sources, targets, sems):
    copies = [
        pltpu.make_async_copy(a, b, sems.at[n]) for n, (a, b) in enumerate(zip(sources, targets))
    ]
    for copy in copies:
        copy.start()
    return copies


def wait(copies):
    for copy in copies:
        copy.wait()


def fetched(*arrays):
    return [pltpu.VMEM(a.shape, a.dtype) for a in arrays] + [
        pltpu.SemaphoreType.DMA((len(arrays),))
    ]


def over_rows(vector, rows):
    tiles = [
        jnp.broadcast_to(vector[c * 128 : (c + 1) * 128], (rows, 128))
        for c in range(vector.shape[0] // 128)
    ]
    return jnp.concatenate(tiles, axis=1)


def smem():
    return pl.BlockSpec(memory_space=pltpu.SMEM)


def cost(flops, nbytes, trans=0):
    return pl.CostEstimate(flops=int(flops), bytes_accessed=int(nbytes), transcendentals=int(trans))


def column(scale, c):
    return jnp.broadcast_to(scale[c * 128 : (c + 1) * 128], (128, 128)).T


def prefix_kernel(place, *rest):
    sources, outs, rest = rest[:3], rest[3 : 3 + SQ], rest[3 + SQ :]
    *parts, scale, keys, values, sems, out_sems = rest
    i = lax.rem(place[0], SQ)

    def leave(half):
        return fetch(
            [parts[half].at[jnp.bitwise_xor(i, m)] for m in range(SQ)],
            [out.at[pl.ds(half * QD, QD), :] for out in outs],
            out_sems.at[half],
        )

    copies = fetch(sources, (scale, keys, values), sems)
    rows = keys.shape[0]
    wait(copies[:2])
    for c in range(D // 128):
        cols = slice(c * 128, (c + 1) * 128)
        scale_t = jnp.concatenate([column(scale, c)] * (rows // 128), axis=1)
        split(parts[0], 0, c, head_unit_t(keys[:, cols].T.astype(f32), scale_t).astype(bf16))
    left = leave(0)
    wait(copies[2:])
    for c in range(D // 128):
        split(parts[1], 0, c, values[:, c * 128 : (c + 1) * 128].T)
    wait(left + leave(1))


def split(out, base, c, block):
    for part in range(0, 128, HEAD):
        row = c * 128 + part
        at = base + row % QD
        out[row // QD, at : at + HEAD, :] = block[part : part + HEAD, :]


def prefix_call(place, scale, keys, values):
    rows = keys.shape[0]
    return pl.pallas_call(
        prefix_kernel,
        out_shape=[jax.ShapeDtypeStruct((2 * QD, rows), bf16)] * SQ,
        in_specs=[smem()] + [hbm()] * 3,
        out_specs=[hbm()] * SQ,
        scratch_shapes=[pltpu.VMEM((SQ, QD, rows), bf16)] * 2
        + fetched(scale, keys, values)
        + [pltpu.SemaphoreType.DMA((2, SQ))],
        compiler_params=params(PREFIX_LIMIT),
        cost_estimate=cost(5e10, 4 * rows * D * 2),
        name="prefix_prep",
    )(place, scale, keys, values)


def qkv_kernel(squares, place, tokens_hbm, scale_hbm, w_hbm, queries, *rest):
    outs, (parts, tokens, scale, sems, weights, w_sems) = rest[:SQ], rest[SQ:]
    small = fetch((tokens_hbm, scale_hbm), (tokens, scale), sems)
    spans = [pl.ds(p * D, D) for p in range(3)]
    copies = fetch([w_hbm.at[:, p] for p in spans], [weights.at[:, p] for p in spans], w_sems)
    wait(small)
    rows = tokens.shape[0]
    hidden = unit(tokens[...].astype(f32)).astype(bf16)
    columns = [column(scale, c)[:, :rows] for c in range(D // 128)]
    for part in range(3):
        copies[part].wait()
        out = jnp.dot(hidden, weights[:, part * D : (part + 1) * D], preferred_element_type=f32)
        for c in range(D // 128):
            block = out[:, c * 128 : (c + 1) * 128].T
            if part < 2:
                block = head_unit_t(block, columns[c])
            if part == 0:
                block = (block * math.sqrt(HEAD)).astype(bf16)
                for s in range(squares):
                    queries[s * D + c * 128 : s * D + (c + 1) * 128, :] = block
            else:
                split(parts, (part - 1) * QD, c, block.astype(bf16))
    i = lax.rem(place[0], SQ)
    for m in range(SQ):
        outs[m][...] = parts[jnp.bitwise_xor(i, m)]


def qkv_call(squares, place, tokens, scale, weights):
    rows = tokens.shape[0]
    pair = jax.ShapeDtypeStruct((2 * QD, rows), bf16)
    return pl.pallas_call(
        functools.partial(qkv_kernel, squares),
        out_shape=[jax.ShapeDtypeStruct((squares * D, rows), bf16)] + [pair] * SQ,
        in_specs=[smem()] + [hbm()] * 3,
        out_specs=[vmem()] * (1 + SQ),
        scratch_shapes=[
            pltpu.VMEM((SQ, 2 * QD, rows), bf16),
            *fetched(tokens, scale),
            pltpu.VMEM((D, 3 * D), bf16),
            pltpu.SemaphoreType.DMA((3,)),
        ],
        compiler_params=params(QKV_LIMIT),
        cost_estimate=cost(5e10, 3 * D * D * 2),
        name="qkv",
    )(place, tokens, scale, weights)


def arrive_kernel(*refs):
    parts, out = refs[:-1], refs[-1]
    out[...] = functools.reduce(jnp.add, [p[:16, :128].astype(f32) for p in parts])


ARRIVE_COST = 20e9


def arrive_call(parts):
    return pl.pallas_call(
        arrive_kernel,
        out_shape=jax.ShapeDtypeStruct((16, 128), f32),
        in_specs=[vmem()] * len(parts),
        out_specs=vmem(),
        compiler_params=params(2),
        cost_estimate=cost(ARRIVE_COST, 0),
        name="arrive",
    )(*parts)


def cached_kernel(query_all, _, *rest):
    prefix, (accum, stats, keys, values) = rest[:SQ], rest[SQ:]
    extent, _, rows = query_all.shape
    span = prefix[0].shape[1]
    for n, part in enumerate(prefix):
        at = slice(n * span, (n + 1) * span)
        for h in range(HQ):
            keys[h, at, :] = part[h * HEAD : (h + 1) * HEAD, :].T
        values[:, at] = part[QD:, :]
    steps = [(s, h) for s in range(extent // SQ) for h in range(HQ)]
    cuts = [slice(k, k + 2 * span) for k in range(0, SQ * span, 2 * span)]

    def queries(s, h):
        head = slice(h * HEAD, (h + 1) * HEAD)
        return jnp.concatenate([query_all[s * SQ + j, head, :] for j in range(SQ)], axis=1)

    def part_scores(h, cut, query):
        return jnp.dot(keys[h, cut, :], query, preferred_element_type=f32)

    query = queries(0, 0)
    scores = [part_scores(0, cut, query) for cut in cuts]
    for n, (s, h) in enumerate(steps):
        head = slice(h * HEAD, (h + 1) * HEAD)
        top = functools.reduce(jnp.maximum, [jnp.max(x, axis=0, keepdims=True) for x in scores])
        following = steps[n + 1] if n + 1 < len(steps) else None
        if following:
            query = queries(*following)
        ahead, total, blended = [], 0.0, 0.0
        for cut, score in zip(cuts, scores):
            if following:
                ahead.append(part_scores(following[1], cut, query))
            weights = jnp.exp(score - top)
            total = total + jnp.sum(weights, axis=0, keepdims=True)
            blended = blended + jnp.dot(
                values[head, cut], weights.astype(bf16), preferred_element_type=f32
            )
        accum[s, head, :] = blended
        stats[s, h : h + 1, :] = top
        stats[s, 8 + h : 9 + h, :] = total
        scores = ahead


def cached_call(queries, arrived, prefix):
    extent, _, rows = queries.shape
    span = prefix[0].shape[1]
    return pl.pallas_call(
        cached_kernel,
        out_shape=[
            jax.ShapeDtypeStruct((extent // SQ, QD, SQ * rows), f32),
            jax.ShapeDtypeStruct((extent // SQ, 16, SQ * rows), f32),
        ],
        in_specs=[vmem()] * (2 + SQ),
        out_specs=[vmem()] * 2,
        scratch_shapes=[
            pltpu.VMEM((HQ, SQ * span, HEAD), bf16),
            pltpu.VMEM((QD, SQ * span), bf16),
        ],
        compiler_params=params(16),
        cost_estimate=cost(CACHED_COST, 0, 0),
        name="attend_cached",
    )(queries, arrived, *prefix)


CACHED_COST = 1e9


def widen(part, lanes, width, fill):
    rows = part.shape[0]
    pieces = []
    if lanes.start:
        pieces.append(jnp.full((rows, lanes.start), fill, f32))
    pieces.append(part)
    if lanes.stop < width:
        pieces.append(jnp.full((rows, width - lanes.stop), fill, f32))
    return jnp.concatenate(pieces, axis=1)


def suffix_kernel(count, place, lengths, query_all, accum, stats, *rest):
    suffix, w_hbm, rest = rest[:SQ], rest[SQ], rest[SQ + 1 :]
    outs, (w_out, pairs, mixes, sems) = rest[:count], rest[count:]
    copies = fetch([w_hbm], [w_out], sems)
    extent, _, rows = query_all.shape
    i = lax.rem(place[0], SQ)
    square = lax.div(place[0], SQ)
    width = SQ * rows
    for m in range(SQ):
        pairs[jnp.bitwise_xor(i, m)] = suffix[m][...]
    for shift in range(extent // SQ):
        query_square = jnp.bitwise_xor(square, shift)
        position = query_square * width + lax.broadcasted_iota(jnp.int32, (1, width), 1)
        first = jnp.zeros((1, width), jnp.int32)
        bound = jnp.int32(0)
        for r in range(lengths.shape[1]):
            bound = bound + lengths[0, r]
            first = jnp.where(position >= bound, bound, first)
        windows = [(SQ - 2, 0, 1), (SQ - 1, 0, 2)]
        if not shift:
            windows = [(j, j, min(SQ, j + 3)) for j in range(SQ)]
        masks = []
        for block, begin, end in windows:
            lanes = slice(begin * rows, end * rows)
            key_at = (square * SQ + block) * rows + lax.broadcasted_iota(
                jnp.int32, (rows, lanes.stop - lanes.start), 0
            )
            allowed = (key_at >= first[:, lanes]) & (key_at <= position[:, lanes])
            masks.append(jnp.where(allowed, 0.0, NEG))
        scores = []
        for h in range(HQ):
            head = slice(h * HEAD, (h + 1) * HEAD)
            query = [query_all[query_square * SQ + j, head, :] for j in range(windows[-1][2])]
            for (block, begin, end), mask in zip(windows, masks):
                score = jnp.dot(
                    pairs[block, head, :].T,
                    jnp.concatenate(query[begin:end], axis=1),
                    preferred_element_type=f32,
                )
                scores.append(score + mask)
        states = []
        for h in range(HQ):
            cached_top = stats[query_square, h : h + 1, :]
            top = cached_top
            part = scores[h * len(windows) : (h + 1) * len(windows)]
            for score, (block, begin, end) in zip(part, windows):
                lanes = slice(begin * rows, end * rows)
                level = jnp.max(score, axis=0, keepdims=True)
                top = jnp.maximum(top, widen(level, lanes, width, NEG))
            shrink = jnp.exp(cached_top - top)
            total = stats[query_square, 8 + h : 9 + h, :] * shrink
            weights = []
            for score, (block, begin, end) in zip(part, windows):
                lanes = slice(begin * rows, end * rows)
                weight = jnp.exp(score - top[:, lanes])
                total = total + widen(jnp.sum(weight, axis=0, keepdims=True), lanes, width, 0.0)
                weights.append(weight.astype(bf16))
            states.append((top, shrink, total, weights))
        for h, (top, shrink, total, weights) in enumerate(states):
            head = slice(h * HEAD, (h + 1) * HEAD)
            head_v = slice(QD + h * HEAD, QD + (h + 1) * HEAD)
            mixed = accum[query_square, head, :] * shrink
            for weight, (block, begin, end) in zip(weights, windows):
                lanes = slice(begin * rows, end * rows)
                blended = jnp.dot(pairs[block, head_v, :], weight, preferred_element_type=f32)
                mixed = mixed + widen(blended, lanes, width, 0.0)
            mixes[head, :] = mixed * (1.0 / total)
            level = top + jnp.log(total)
            high = level.astype(bf16).astype(f32)
            middle = (level - high).astype(bf16).astype(f32)
            for n, piece in enumerate((high, middle, level - high - middle)):
                row = QD + n * HQ + h
                mixes[row : row + 1, :] = piece
        mixes[QD + LSE - 1 :, :] = jnp.zeros((1, width), f32)
        for m in range(SQ):
            lanes = pl.ds(pl.multiple_of(jnp.bitwise_xor(i, m) * rows, rows), rows)
            outs[shift * SQ + m][...] = mixes[:, lanes].astype(bf16)
    wait(copies)


def suffix_call(place, lengths, queries, accum, stats, suffix, w_out):
    extent, _, rows = queries.shape
    return pl.pallas_call(
        functools.partial(suffix_kernel, extent),
        out_shape=[jax.ShapeDtypeStruct((QD + LSE, rows), bf16)] * extent
        + [jax.ShapeDtypeStruct(w_out.shape, bf16)],
        in_specs=[smem(), smem()] + [vmem()] * (3 + SQ) + [hbm()],
        out_specs=[vmem()] * (extent + 1),
        scratch_shapes=[
            pltpu.VMEM((SQ, 2 * QD, rows), bf16),
            pltpu.VMEM((QD + LSE, SQ * rows), f32),
            pltpu.SemaphoreType.DMA((1,)),
        ],
        compiler_params=params(8),
        cost_estimate=cost(2e10, 8 * MIB, 0),
        name="attend_suffix",
    )(place, lengths, queries, accum, stats, *suffix, w_out)


def project_kernel(order, place, tokens_hbm, rate_hbm, w_out, *rest):
    count = len(order)
    arrived, rest = rest[:count], rest[count:]
    hidden_out, flat_out, mix, tokens, rate, sems = rest
    copies = fetch((tokens_hbm, rate_hbm), (tokens, rate), sems)
    squares = count // SQ
    i = lax.rem(place[0], SQ)
    parts = dict(zip(order, arrived))
    for m in range(SQ):
        group = [parts[s * SQ + m] for s in range(squares)]
        start = jnp.bitwise_xor(i, m) * QD
        levels = []
        for part in group:
            pieces = part[QD:, :].astype(f32)
            levels.append(pieces[:HQ] + pieces[HQ : 2 * HQ] + pieces[2 * HQ : 3 * HQ])
        top = functools.reduce(jnp.maximum, levels)
        weights = [jnp.exp(v - top) for v in levels]
        inverse = 1.0 / functools.reduce(jnp.add, weights)
        weights = [w * inverse for w in weights]
        for h in range(HQ):
            head = slice(h * HEAD, (h + 1) * HEAD)
            mixed = functools.reduce(
                jnp.add, [w[h : h + 1, :] * p[head, :].astype(f32) for w, p in zip(weights, group)]
            )
            at = pl.multiple_of(start + h * HEAD, HEAD)
            mix[pl.ds(at, HEAD), :] = mixed.astype(bf16)
    wait(copies)
    hidden = unit(tokens[...].astype(f32))
    attn = jnp.concatenate(
        [mix[c * 128 : (c + 1) * 128, :].astype(f32).T.astype(bf16) for c in range(D // 128)], axis=1
    )
    attended = unit(jnp.dot(attn, w_out[...], preferred_element_type=f32))
    hidden = unit(hidden + over_rows(rate, hidden.shape[0]) * (attended - hidden))
    hidden_out[...] = hidden
    flat_out[...] = hidden.astype(bf16)


def project_call(place, tokens, rate, w_out, parts):
    rows = tokens.shape[0]
    return pl.pallas_call(
        functools.partial(project_kernel, list(parts)),
        out_shape=[jax.ShapeDtypeStruct((rows, D), f32), jax.ShapeDtypeStruct((rows, D), bf16)],
        in_specs=[smem(), hbm(), hbm()] + [vmem()] * (1 + len(parts)),
        out_specs=[vmem()] * 2,
        scratch_shapes=[
            pltpu.VMEM((D, rows), bf16),
            *fetched(tokens, rate),
        ],
        compiler_params=params(8),
        cost_estimate=cost(2 * rows * D * D, D * D * 2),
        name="project",
    )(place, tokens, rate, w_out, *parts.values())


def mlp_kernel(first, second, w_up, w_gate, w_down, up_scale, gate_scale, keep, send):
    rows = first.shape[0]
    data = jnp.concatenate([first[...], second[...]], axis=0)
    up = jnp.dot(data, w_up[...], preferred_element_type=f32) * over_rows(up_scale, 2 * rows)
    gate = jnp.dot(data, w_gate[...], preferred_element_type=f32)
    gate = gate * (over_rows(gate_scale, 2 * rows) * math.sqrt(D))
    act = (up * (gate / (1.0 + jnp.exp(-gate)))).astype(bf16)
    part = jnp.dot(act, w_down[...], preferred_element_type=f32)
    keep[...] = part[:rows, :]
    send[...] = part[rows:, :].astype(bf16)


def mlp_call(first, second, weights):
    rows = first.shape[0]
    units = weights[0].shape[1]
    return pl.pallas_call(
        mlp_kernel,
        out_shape=[jax.ShapeDtypeStruct((rows, D), f32), jax.ShapeDtypeStruct((rows, D), bf16)],
        in_specs=[vmem()] * 7,
        out_specs=[vmem()] * 2,
        compiler_params=params(12),
        cost_estimate=cost(2 * 2 * rows * D * units * 3, 3 * D * units * 2, 2 * rows * units),
        name="mlp",
    )(first, second, *weights)


def add_kernel(kept, arrived, out):
    out[...] = (kept[...] + arrived[...].astype(f32)).astype(bf16)


def add_call(kept, arrived):
    return pl.pallas_call(
        add_kernel,
        out_shape=jax.ShapeDtypeStruct(kept.shape, bf16),
        in_specs=[vmem()] * 2,
        out_specs=vmem(),
        compiler_params=params(8),
        cost_estimate=cost(kept.size, kept.size * 8),
        name="add_partials",
    )(kept, arrived)


def final_kernel(hidden, rate_hbm, kept, *rest):
    arrived, (out, rate, sems) = rest[:-3], rest[-3:]
    copies = fetch([rate_hbm], [rate], sems)
    total = kept[...]
    for part in arrived:
        total = total + part[...].astype(f32)
    state = hidden[...]
    wait(copies)
    state = unit(state + over_rows(rate, state.shape[0]) * (unit(total) - state))
    out[...] = (math.sqrt(D) * state).astype(bf16)


def final_call(hidden, rate, kept, arrived):
    return pl.pallas_call(
        final_kernel,
        out_shape=jax.ShapeDtypeStruct(hidden.shape, bf16),
        in_specs=[vmem(), hbm()] + [vmem()] * (1 + len(arrived)),
        out_specs=pl.BlockSpec(hidden.shape, lambda: (0, 0)),
        scratch_shapes=fetched(rate),
        compiler_params=params(8),
        cost_estimate=cost(hidden.size * 10, hidden.size * 12),
        name="finish",
    )(hidden, rate, kept, *arrived)


def swap(shard, axis, mask):
    length = lax.axis_size(axis)
    return lax.ppermute(shard, axis, [(j, j ^ mask) for j in range(length)])


def body(
    tokens,
    seg_lengths,
    prefix_keys,
    prefix_values,
    w_qkv,
    w_out,
    qk_scale,
    attn_rate,
    w_up,
    w_gate,
    w_down,
    up_scale,
    gate_scale,
    mlp_rate,
):
    extent = lax.axis_size("tok")
    squares = extent // SQ
    place = lax.axis_index("tok").astype(jnp.int32).reshape(1)
    own = tokens[0]
    rows = own.shape[0]

    cached = prefix_call(place, qk_scale, prefix_keys[0], prefix_values[0])
    prefix = [cached[0]] + [swap(cached[m], "tok", m) for m in range(1, SQ)]
    queries, *sent = qkv_call(squares, place, own, qk_scale, w_qkv)
    suffix = [sent[0]] + [swap(sent[m], "tok", m) for m in range(1, SQ)]
    queries = lax.all_to_all(queries.reshape(extent, QD, rows), "tok", 0, 0)
    accum, stats = cached_call(queries, arrive_call(prefix), prefix)
    *parts, w_out = suffix_call(place, seg_lengths, queries, accum, stats, suffix, w_out)
    order = [1, *range(SQ, extent), *range(SQ - 1, 1, -1)]
    parts = {m: swap(parts[m], "tok", m) for m in order} | {0: parts[0]}
    hidden, flat = project_call(place, own, attn_rate, w_out, parts)

    weights = (w_up, w_gate, w_down, up_scale, gate_scale)
    chips = lax.axis_size("grp") // 2
    remote = [swap(flat, "grp", 2 * c) for c in range(1, chips)]
    keep, send = mlp_call(flat, swap(flat, "grp", 1), weights)
    arrived = [swap(send, "grp", 1)]
    for c in range(1, chips):
        data, keep = lax.optimization_barrier((remote[c - 1], keep))
        kept, send = mlp_call(data, swap(data, "grp", 1), weights)
        arrived.append(swap(add_call(kept, swap(send, "grp", 1)), "grp", 2 * c))
    return final_call(hidden, mlp_rate, keep, arrived)[None]


def solution(mesh):
    in_specs = (
        P("grp", "tok", None),
        P("grp", None),
        P("grp", "tok", None),
        P("grp", "tok", None),
        P(),
        P(),
        P(),
        P(),
        P(None, "grp"),
        P(None, "grp"),
        P("grp", None),
        P("grp"),
        P("grp"),
        P(),
    )
    out_specs = P("grp", "tok", None)
    return jax.shard_map(body, mesh=mesh, in_specs=in_specs, out_specs=out_specs, check_vma=False)
```

```python
import functools
import math

import jax
import jax.numpy as jnp
from jax import lax
from jax.experimental import pallas as pl
from jax.experimental.pallas import tpu as pltpu
from jax.sharding import PartitionSpec as P

D = 1280
HEADS = 20
HEAD = 64
EPS = 1e-06
SQ = 4
HQ = HEADS // SQ
QD = HQ * HEAD
LSE = 16
NEG = -1e30
PREFIX_LIMIT = 61
QKV_LIMIT = 50
MIB = 1 << 20

f32 = jnp.float32
bf16 = jnp.bfloat16


def unit(vector):
    return vector * lax.rsqrt(jnp.sum(vector * vector, axis=-1, keepdims=True) + EPS)


def head_unit_t(block, scale):
    dims, rows = block.shape
    per_head = block.reshape(dims // HEAD, HEAD, rows)
    total = jnp.sum(per_head * per_head, axis=1, keepdims=True)
    return (per_head * lax.rsqrt(total + EPS)).reshape(dims, rows) * scale


def params(limit):
    return pltpu.CompilerParams(vmem_limit_bytes=limit * MIB)


def vmem():
    return pl.BlockSpec(memory_space=pltpu.VMEM)


def hbm():
    return pl.BlockSpec(memory_space=pltpu.HBM)


def fetch(sources, targets, sems):
    copies = [
        pltpu.make_async_copy(a, b, sems.at[n]) for n, (a, b) in enumerate(zip(sources, targets))
    ]
    for copy in copies:
        copy.start()
    return copies


def wait(copies):
    for copy in copies:
        copy.wait()


def fetched(*arrays):
    return [pltpu.VMEM(a.shape, a.dtype) for a in arrays] + [
        pltpu.SemaphoreType.DMA((len(arrays),))
    ]


def over_rows(vector, rows):
    tiles = [
        jnp.broadcast_to(vector[c * 128 : (c + 1) * 128], (rows, 128))
        for c in range(vector.shape[0] // 128)
    ]
    return jnp.concatenate(tiles, axis=1)


def smem():
    return pl.BlockSpec(memory_space=pltpu.SMEM)


def cost(flops, nbytes, trans=0):
    return pl.CostEstimate(flops=int(flops), bytes_accessed=int(nbytes), transcendentals=int(trans))


def column(scale, c):
    return jnp.broadcast_to(scale[c * 128 : (c + 1) * 128], (128, 128)).T


def prefix_kernel(place, *rest):
    sources, outs, rest = rest[:3], rest[3 : 3 + SQ], rest[3 + SQ :]
    *parts, scale, keys, values, sems, out_sems = rest
    i = lax.rem(place[0], SQ)

    def leave(half):
        return fetch(
            [parts[half].at[jnp.bitwise_xor(i, m)] for m in range(SQ)],
            [out.at[pl.ds(half * QD, QD), :] for out in outs],
            out_sems.at[half],
        )

    copies = fetch(sources, (scale, keys, values), sems)
    rows = keys.shape[0]
    wait(copies[:2])
    for c in range(D // 128):
        cols = slice(c * 128, (c + 1) * 128)
        scale_t = jnp.concatenate([column(scale, c)] * (rows // 128), axis=1)
        split(parts[0], 0, c, head_unit_t(keys[:, cols].T.astype(f32), scale_t).astype(bf16))
    left = leave(0)
    wait(copies[2:])
    for c in range(D // 128):
        split(parts[1], 0, c, values[:, c * 128 : (c + 1) * 128].T)
    wait(left + leave(1))


def split(out, base, c, block):
    for part in range(0, 128, HEAD):
        row = c * 128 + part
        at = base + row % QD
        out[row // QD, at : at + HEAD, :] = block[part : part + HEAD, :]


def prefix_call(place, scale, keys, values):
    rows = keys.shape[0]
    return pl.pallas_call(
        prefix_kernel,
        out_shape=[jax.ShapeDtypeStruct((2 * QD, rows), bf16)] * SQ,
        in_specs=[smem()] + [hbm()] * 3,
        out_specs=[hbm()] * SQ,
        scratch_shapes=[pltpu.VMEM((SQ, QD, rows), bf16)] * 2
        + fetched(scale, keys, values)
        + [pltpu.SemaphoreType.DMA((2, SQ))],
        compiler_params=params(PREFIX_LIMIT),
        cost_estimate=cost(5e10, 4 * rows * D * 2),
        name="prefix_prep",
    )(place, scale, keys, values)


def qkv_kernel(squares, place, tokens_hbm, scale_hbm, w_hbm, queries, *rest):
    outs, (parts, tokens, scale, sems, weights, w_sems) = rest[:SQ], rest[SQ:]
    small = fetch((tokens_hbm, scale_hbm), (tokens, scale), sems)
    spans = [pl.ds(p * D, D) for p in range(3)]
    copies = fetch([w_hbm.at[:, p] for p in spans], [weights.at[:, p] for p in spans], w_sems)
    wait(small)
    rows = tokens.shape[0]
    hidden = unit(tokens[...].astype(f32)).astype(bf16)
    columns = [column(scale, c)[:, :rows] for c in range(D // 128)]
    for part in range(3):
        copies[part].wait()
        out = jnp.dot(hidden, weights[:, part * D : (part + 1) * D], preferred_element_type=f32)
        for c in range(D // 128):
            block = out[:, c * 128 : (c + 1) * 128].T
            if part < 2:
                block = head_unit_t(block, columns[c])
            if part == 0:
                block = (block * math.sqrt(HEAD)).astype(bf16)
                for s in range(squares):
                    queries[s * D + c * 128 : s * D + (c + 1) * 128, :] = block
            else:
                split(parts, (part - 1) * QD, c, block.astype(bf16))
    i = lax.rem(place[0], SQ)
    for m in range(SQ):
        outs[m][...] = parts[jnp.bitwise_xor(i, m)]


def qkv_call(squares, place, tokens, scale, weights):
    rows = tokens.shape[0]
    pair = jax.ShapeDtypeStruct((2 * QD, rows), bf16)
    return pl.pallas_call(
        functools.partial(qkv_kernel, squares),
        out_shape=[jax.ShapeDtypeStruct((squares * D, rows), bf16)] + [pair] * SQ,
        in_specs=[smem()] + [hbm()] * 3,
        out_specs=[vmem()] * (1 + SQ),
        scratch_shapes=[
            pltpu.VMEM((SQ, 2 * QD, rows), bf16),
            *fetched(tokens, scale),
            pltpu.VMEM((D, 3 * D), bf16),
            pltpu.SemaphoreType.DMA((3,)),
        ],
        compiler_params=params(QKV_LIMIT),
        cost_estimate=cost(5e10, 3 * D * D * 2),
        name="qkv",
    )(place, tokens, scale, weights)


def arrive_kernel(*refs):
    parts, out = refs[:-1], refs[-1]
    out[...] = functools.reduce(jnp.add, [p[:16, :128].astype(f32) for p in parts])


ARRIVE_COST = 20e9


def arrive_call(parts):
    return pl.pallas_call(
        arrive_kernel,
        out_shape=jax.ShapeDtypeStruct((16, 128), f32),
        in_specs=[vmem()] * len(parts),
        out_specs=vmem(),
        compiler_params=params(2),
        cost_estimate=cost(ARRIVE_COST, 0),
        name="arrive",
    )(*parts)


def cached_kernel(query_all, _, *rest):
    prefix, (accum, stats, keys, values) = rest[:SQ], rest[SQ:]
    extent, _, rows = query_all.shape
    span = prefix[0].shape[1]
    for n, part in enumerate(prefix):
        at = slice(n * span, (n + 1) * span)
        for h in range(HQ):
            keys[h, at, :] = part[h * HEAD : (h + 1) * HEAD, :].T
        values[:, at] = part[QD:, :]
    steps = [(s, h) for s in range(extent // SQ) for h in range(HQ)]
    cuts = [slice(k, k + 2 * span) for k in range(0, SQ * span, 2 * span)]

    def queries(s, h):
        head = slice(h * HEAD, (h + 1) * HEAD)
        return jnp.concatenate([query_all[s * SQ + j, head, :] for j in range(SQ)], axis=1)

    def part_scores(h, cut, query):
        return jnp.dot(keys[h, cut, :], query, preferred_element_type=f32)

    query = queries(0, 0)
    scores = [part_scores(0, cut, query) for cut in cuts]
    for n, (s, h) in enumerate(steps):
        head = slice(h * HEAD, (h + 1) * HEAD)
        top = functools.reduce(jnp.maximum, [jnp.max(x, axis=0, keepdims=True) for x in scores])
        following = steps[n + 1] if n + 1 < len(steps) else None
        if following:
            query = queries(*following)
        ahead, total, blended = [], 0.0, 0.0
        for cut, score in zip(cuts, scores):
            if following:
                ahead.append(part_scores(following[1], cut, query))
            weights = jnp.exp(score - top)
            total = total + jnp.sum(weights, axis=0, keepdims=True)
            blended = blended + jnp.dot(
                values[head, cut], weights.astype(bf16), preferred_element_type=f32
            )
        accum[s, head, :] = blended
        stats[s, h : h + 1, :] = top
        stats[s, 8 + h : 9 + h, :] = total
        scores = ahead


def cached_call(queries, arrived, prefix):
    extent, _, rows = queries.shape
    span = prefix[0].shape[1]
    return pl.pallas_call(
        cached_kernel,
        out_shape=[
            jax.ShapeDtypeStruct((extent // SQ, QD, SQ * rows), f32),
            jax.ShapeDtypeStruct((extent // SQ, 16, SQ * rows), f32),
        ],
        in_specs=[vmem()] * (2 + SQ),
        out_specs=[vmem()] * 2,
        scratch_shapes=[
            pltpu.VMEM((HQ, SQ * span, HEAD), bf16),
            pltpu.VMEM((QD, SQ * span), bf16),
        ],
        compiler_params=params(16),
        cost_estimate=cost(CACHED_COST, 0, 0),
        name="attend_cached",
    )(queries, arrived, *prefix)


CACHED_COST = 1e9


def widen(part, lanes, width, fill):
    rows = part.shape[0]
    pieces = []
    if lanes.start:
        pieces.append(jnp.full((rows, lanes.start), fill, f32))
    pieces.append(part)
    if lanes.stop < width:
        pieces.append(jnp.full((rows, width - lanes.stop), fill, f32))
    return jnp.concatenate(pieces, axis=1)


def suffix_kernel(count, place, lengths, query_all, accum, stats, *rest):
    suffix, w_hbm, rest = rest[:SQ], rest[SQ], rest[SQ + 1 :]
    outs, (w_out, pairs, mixes, sems) = rest[:count], rest[count:]
    copies = fetch([w_hbm], [w_out], sems)
    extent, _, rows = query_all.shape
    i = lax.rem(place[0], SQ)
    square = lax.div(place[0], SQ)
    width = SQ * rows
    for m in range(SQ):
        pairs[jnp.bitwise_xor(i, m)] = suffix[m][...]
    for shift in range(extent // SQ):
        query_square = jnp.bitwise_xor(square, shift)
        position = query_square * width + lax.broadcasted_iota(jnp.int32, (1, width), 1)
        first = jnp.zeros((1, width), jnp.int32)
        bound = jnp.int32(0)
        for r in range(lengths.shape[1]):
            bound = bound + lengths[0, r]
            first = jnp.where(position >= bound, bound, first)
        windows = [(SQ - 2, 0, 1), (SQ - 1, 0, 2)]
        if not shift:
            windows = [(j, j, min(SQ, j + 3)) for j in range(SQ)]
        masks = []
        for block, begin, end in windows:
            lanes = slice(begin * rows, end * rows)
            key_at = (square * SQ + block) * rows + lax.broadcasted_iota(
                jnp.int32, (rows, lanes.stop - lanes.start), 0
            )
            allowed = (key_at >= first[:, lanes]) & (key_at <= position[:, lanes])
            masks.append(jnp.where(allowed, 0.0, NEG))
        scores = []
        for h in range(HQ):
            head = slice(h * HEAD, (h + 1) * HEAD)
            query = [query_all[query_square * SQ + j, head, :] for j in range(windows[-1][2])]
            for (block, begin, end), mask in zip(windows, masks):
                score = jnp.dot(
                    pairs[block, head, :].T,
                    jnp.concatenate(query[begin:end], axis=1),
                    preferred_element_type=f32,
                )
                scores.append(score + mask)
        states = []
        for h in range(HQ):
            cached_top = stats[query_square, h : h + 1, :]
            top = cached_top
            part = scores[h * len(windows) : (h + 1) * len(windows)]
            for score, (block, begin, end) in zip(part, windows):
                lanes = slice(begin * rows, end * rows)
                level = jnp.max(score, axis=0, keepdims=True)
                top = jnp.maximum(top, widen(level, lanes, width, NEG))
            shrink = jnp.exp(cached_top - top)
            total = stats[query_square, 8 + h : 9 + h, :] * shrink
            weights = []
            for score, (block, begin, end) in zip(part, windows):
                lanes = slice(begin * rows, end * rows)
                weight = jnp.exp(score - top[:, lanes])
                total = total + widen(jnp.sum(weight, axis=0, keepdims=True), lanes, width, 0.0)
                weights.append(weight.astype(bf16))
            states.append((top, shrink, total, weights))
        for h, (top, shrink, total, weights) in enumerate(states):
            head = slice(h * HEAD, (h + 1) * HEAD)
            head_v = slice(QD + h * HEAD, QD + (h + 1) * HEAD)
            mixed = accum[query_square, head, :] * shrink
            for weight, (block, begin, end) in zip(weights, windows):
                lanes = slice(begin * rows, end * rows)
                blended = jnp.dot(pairs[block, head_v, :], weight, preferred_element_type=f32)
                mixed = mixed + widen(blended, lanes, width, 0.0)
            mixes[head, :] = mixed * (1.0 / total)
            level = top + jnp.log(total)
            high = level.astype(bf16).astype(f32)
            middle = (level - high).astype(bf16).astype(f32)
            for n, piece in enumerate((high, middle, level - high - middle)):
                row = QD + n * HQ + h
                mixes[row : row + 1, :] = piece
        mixes[QD + LSE - 1 :, :] = jnp.zeros((1, width), f32)
        for m in range(SQ):
            lanes = pl.ds(pl.multiple_of(jnp.bitwise_xor(i, m) * rows, rows), rows)
            outs[shift * SQ + m][...] = mixes[:, lanes].astype(bf16)
    wait(copies)


def suffix_call(place, lengths, queries, accum, stats, suffix, w_out):
    extent, _, rows = queries.shape
    return pl.pallas_call(
        functools.partial(suffix_kernel, extent),
        out_shape=[jax.ShapeDtypeStruct((QD + LSE, rows), bf16)] * extent
        + [jax.ShapeDtypeStruct(w_out.shape, bf16)],
        in_specs=[smem(), smem()] + [vmem()] * (3 + SQ) + [hbm()],
        out_specs=[vmem()] * (extent + 1),
        scratch_shapes=[
            pltpu.VMEM((SQ, 2 * QD, rows), bf16),
            pltpu.VMEM((QD + LSE, SQ * rows), f32),
            pltpu.SemaphoreType.DMA((1,)),
        ],
        compiler_params=params(8),
        cost_estimate=cost(2e10, 8 * MIB, 0),
        name="attend_suffix",
    )(place, lengths, queries, accum, stats, *suffix, w_out)


def project_kernel(order, place, tokens_hbm, rate_hbm, w_out, *rest):
    count = len(order)
    arrived, rest = rest[:count], rest[count:]
    hidden_out, flat_out, mix, tokens, rate, sems = rest
    copies = fetch((tokens_hbm, rate_hbm), (tokens, rate), sems)
    squares = count // SQ
    i = lax.rem(place[0], SQ)
    parts = dict(zip(order, arrived))
    for m in range(SQ):
        group = [parts[s * SQ + m] for s in range(squares)]
        start = jnp.bitwise_xor(i, m) * QD
        levels = []
        for part in group:
            pieces = part[QD:, :].astype(f32)
            levels.append(pieces[:HQ] + pieces[HQ : 2 * HQ] + pieces[2 * HQ : 3 * HQ])
        top = functools.reduce(jnp.maximum, levels)
        weights = [jnp.exp(v - top) for v in levels]
        inverse = 1.0 / functools.reduce(jnp.add, weights)
        weights = [w * inverse for w in weights]
        for h in range(HQ):
            head = slice(h * HEAD, (h + 1) * HEAD)
            mixed = functools.reduce(
                jnp.add, [w[h : h + 1, :] * p[head, :].astype(f32) for w, p in zip(weights, group)]
            )
            at = pl.multiple_of(start + h * HEAD, HEAD)
            mix[pl.ds(at, HEAD), :] = mixed.astype(bf16)
    wait(copies)
    hidden = unit(tokens[...].astype(f32))
    attn = jnp.concatenate(
        [mix[c * 128 : (c + 1) * 128, :].astype(f32).T.astype(bf16) for c in range(D // 128)], axis=1
    )
    attended = unit(jnp.dot(attn, w_out[...], preferred_element_type=f32))
    hidden = unit(hidden + over_rows(rate, hidden.shape[0]) * (attended - hidden))
    hidden_out[...] = hidden
    flat_out[...] = hidden.astype(bf16)


def project_call(place, tokens, rate, w_out, parts):
    rows = tokens.shape[0]
    return pl.pallas_call(
        functools.partial(project_kernel, list(parts)),
        out_shape=[jax.ShapeDtypeStruct((rows, D), f32), jax.ShapeDtypeStruct((rows, D), bf16)],
        in_specs=[smem(), hbm(), hbm()] + [vmem()] * (1 + len(parts)),
        out_specs=[vmem()] * 2,
        scratch_shapes=[
            pltpu.VMEM((D, rows), bf16),
            *fetched(tokens, rate),
        ],
        compiler_params=params(8),
        cost_estimate=cost(2 * rows * D * D, D * D * 2),
        name="project",
    )(place, tokens, rate, w_out, *parts.values())


def mlp_kernel(first, second, w_up, w_gate, w_down, up_scale, gate_scale, keep, send):
    rows = first.shape[0]
    data = jnp.concatenate([first[...], second[...]], axis=0)
    gate = jnp.dot(data, w_gate[...], preferred_element_type=f32)
    gate = gate * (over_rows(gate_scale, 2 * rows) * math.sqrt(D))
    gate = gate / (1.0 + jnp.exp(-gate))
    up = jnp.dot(data, w_up[...], preferred_element_type=f32) * over_rows(up_scale, 2 * rows)
    act = (up * gate).astype(bf16)
    part = jnp.dot(act, w_down[...], preferred_element_type=f32)
    keep[...] = part[:rows, :]
    send[...] = part[rows:, :].astype(bf16)


def mlp_call(first, second, weights):
    rows = first.shape[0]
    units = weights[0].shape[1]
    return pl.pallas_call(
        mlp_kernel,
        out_shape=[jax.ShapeDtypeStruct((rows, D), f32), jax.ShapeDtypeStruct((rows, D), bf16)],
        in_specs=[vmem()] * 7,
        out_specs=[vmem()] * 2,
        compiler_params=params(12),
        cost_estimate=cost(2 * 2 * rows * D * units * 3, 3 * D * units * 2, 2 * rows * units),
        name="mlp",
    )(first, second, *weights)


def add_kernel(kept, arrived, out):
    out[...] = (kept[...] + arrived[...].astype(f32)).astype(bf16)


def add_call(kept, arrived):
    return pl.pallas_call(
        add_kernel,
        out_shape=jax.ShapeDtypeStruct(kept.shape, bf16),
        in_specs=[vmem()] * 2,
        out_specs=vmem(),
        compiler_params=params(8),
        cost_estimate=cost(kept.size, kept.size * 8),
        name="add_partials",
    )(kept, arrived)


def final_kernel(hidden, rate_hbm, kept, *rest):
    arrived, (out, rate, sems) = rest[:-3], rest[-3:]
    copies = fetch([rate_hbm], [rate], sems)
    total = kept[...]
    for part in arrived:
        total = total + part[...].astype(f32)
    state = hidden[...]
    wait(copies)
    state = unit(state + over_rows(rate, state.shape[0]) * (unit(total) - state))
    out[...] = (math.sqrt(D) * state).astype(bf16)


def final_call(hidden, rate, kept, arrived):
    return pl.pallas_call(
        final_kernel,
        out_shape=jax.ShapeDtypeStruct(hidden.shape, bf16),
        in_specs=[vmem(), hbm()] + [vmem()] * (1 + len(arrived)),
        out_specs=pl.BlockSpec(hidden.shape, lambda: (0, 0)),
        scratch_shapes=fetched(rate),
        compiler_params=params(8),
        cost_estimate=cost(hidden.size * 10, hidden.size * 12),
        name="finish",
    )(hidden, rate, kept, *arrived)


def swap(shard, axis, mask):
    length = lax.axis_size(axis)
    return lax.ppermute(shard, axis, [(j, j ^ mask) for j in range(length)])


def body(
    tokens,
    seg_lengths,
    prefix_keys,
    prefix_values,
    w_qkv,
    w_out,
    qk_scale,
    attn_rate,
    w_up,
    w_gate,
    w_down,
    up_scale,
    gate_scale,
    mlp_rate,
):
    extent = lax.axis_size("tok")
    squares = extent // SQ
    place = lax.axis_index("tok").astype(jnp.int32).reshape(1)
    own = tokens[0]
    rows = own.shape[0]

    cached = prefix_call(place, qk_scale, prefix_keys[0], prefix_values[0])
    prefix = [cached[0]] + [swap(cached[m], "tok", m) for m in range(1, SQ)]
    queries, *sent = qkv_call(squares, place, own, qk_scale, w_qkv)
    suffix = [sent[0]] + [swap(sent[m], "tok", m) for m in range(1, SQ)]
    queries = lax.all_to_all(queries.reshape(extent, QD, rows), "tok", 0, 0)
    accum, stats = cached_call(queries, arrive_call(prefix), prefix)
    *parts, w_out = suffix_call(place, seg_lengths, queries, accum, stats, suffix, w_out)
    order = [1, *range(SQ, extent), *range(SQ - 1, 1, -1)]
    parts = {m: swap(parts[m], "tok", m) for m in order} | {0: parts[0]}
    hidden, flat = project_call(place, own, attn_rate, w_out, parts)

    weights = (w_up, w_gate, w_down, up_scale, gate_scale)
    chips = lax.axis_size("grp") // 2
    remote = [swap(flat, "grp", 2 * c) for c in range(1, chips)]
    keep, send = mlp_call(flat, swap(flat, "grp", 1), weights)
    arrived = [swap(send, "grp", 1)]
    for c in range(1, chips):
        data, keep = lax.optimization_barrier((remote[c - 1], keep))
        kept, send = mlp_call(data, swap(data, "grp", 1), weights)
        arrived.append(swap(add_call(kept, swap(send, "grp", 1)), "grp", 2 * c))
    return final_call(hidden, mlp_rate, keep, arrived)[None]


def solution(mesh):
    in_specs = (
        P("grp", "tok", None),
        P("grp", None),
        P("grp", "tok", None),
        P("grp", "tok", None),
        P(),
        P(),
        P(),
        P(),
        P(None, "grp"),
        P(None, "grp"),
        P("grp", None),
        P("grp"),
        P("grp"),
        P(),
    )
    out_specs = P("grp", "tok", None)
    return jax.shard_map(body, mesh=mesh, in_specs=in_specs, out_specs=out_specs, check_vma=False)
```
